512 devices in a mesh: remap: 2 (over core), grid: 256 (over z, y, x).
Axes of the slice: x: 4, y: 8, z: 8, core: 2. Of those that a mesh axis runs over, the one named last changes fastest.
Arguments:
- tensor: bfloat16 [256, 256, 128, 128], P('grid', None, 'remap'), may hold values from -0.5 to 0.5
- go_blocks: bfloat16 [256, 2, 128, 128], P('grid'), may hold values from -0.5 to 0.5
- gv_blocks: bfloat16 [256, 2, 128, 128], P('grid'), may hold values from -0.5 to 0.5
- partners: int32 [256, 2], P('grid'), may hold values from 0 to 255, as said below
Outputs:
- chi: float32 [256, 2, 256, 256], P('grid', None, 'remap')
The draws below stay inside these ranges and needn't reach their ends.
Inputs may be any that keep to these rules, and one draw needn't show every extreme that they name: `partners`: the 2 entries of a row are distinct blocks; block b belongs to grid index b, and each partner's grid index is at most 1 away from its block's, counted cyclically.
All inputs are finite; a program needn't handle non-finite values.
Results may differ from the reference program's by a relative error of at most 0.004.
Values may be sent and summed in bfloat16 or wider, within the bound.
A program may use at most 128 MiB of HBM per device.

```python
import jax
import jax.numpy as jnp
from jax import lax

BS = 128
ABLK = 1
RI = 256
C = 2
REACH = 1
NBLK = 256


def draw_partners(key, part):
    key = jax.random.fold_in(key, 7)
    blocks = jnp.arange(NBLK)
    owners = blocks // ABLK
    window = (2 * REACH + 1) * ABLK
    places = jnp.arange(window)
    offsets = places // ABLK - REACH
    within = places % ABLK
    grid_count = NBLK // ABLK
    candidates = (owners[:, None] + offsets[None, :]) % grid_count * ABLK + within[None, :]
    scores = jax.random.randint(key, (NBLK, window), 0, 1 << 18) * 64 + places[None, :]
    ranking = jnp.argsort(scores, axis=1)
    return jnp.take_along_axis(candidates, ranking[:, :C], axis=1).astype(jnp.int32)


def steps_of(stream_key, extent, shards, low, high):
    level = 1.0
    for axis_at, parts in shards:
        heights = jax.random.uniform(jax.random.fold_in(jax.random.fold_in(stream_key, 6), axis_at), (parts,), jnp.float32, low / len(shards), high / len(shards))
        level = level * jnp.repeat(jnp.exp(heights), extent[axis_at] // parts).reshape((-1,) + (1,) * (len(extent) - 1 - axis_at))
    return level


def bell_draw(key, shape, deviation, bound, split=(), held_as=jnp.bfloat16):
    level = steps_of(key, shape, split, -0.22, 0.18) if split else 1.0
    values = jax.random.normal(key, shape, jnp.float32) * deviation * level
    return jnp.minimum(jnp.maximum(values, -bound), bound).astype(held_as)


def setup_inputs(seed: int = 0) -> dict:
    splits = jax.random.split(jax.random.key(seed), 5)
    return {
        "tensor": bell_draw(splits[0], (NBLK, RI, BS, BS), (BS ** -0.5), 0.5, ((0, 256), (2, 2))),
        "go_blocks": bell_draw(splits[1], (NBLK, C, BS, BS), BS ** -0.5, 0.5, ((0, 256),)),
        "gv_blocks": bell_draw(splits[2], (NBLK, C, BS, BS), BS ** -0.5, 0.5, ((0, 256),)),
        "partners": draw_partners(jax.random.fold_in(splits[4], 71), 0),
    }


def reference(tensor, go_blocks, gv_blocks, partners):
    def one_block(block_id):
        own_block = tensor[block_id]

        def one_slot(slot_id):
            other_block = tensor[partners[block_id, slot_id]]
            occupied = jnp.dot(own_block.reshape(RI * BS, BS), go_blocks[block_id, slot_id], preferred_element_type=jnp.float32).astype(jnp.bfloat16)
            occupied = occupied.reshape(RI, BS * BS)
            virtual = jnp.dot(other_block.reshape(RI * BS, BS), gv_blocks[block_id, slot_id], preferred_element_type=jnp.float32).astype(jnp.bfloat16)
            swapped = jnp.swapaxes(virtual.reshape(RI, BS, BS), 1, 2).reshape(RI, BS * BS)
            return jnp.dot(occupied, swapped.T, preferred_element_type=jnp.float32)

        return lax.map(one_slot, jnp.arange(C))

    return lax.map(one_block, jnp.arange(NBLK))
```

```python
import jax
import jax.numpy as jnp
from jax import lax
from jax.experimental import pallas as pl
from jax.experimental.pallas import tpu as pltpu
from jax.sharding import PartitionSpec as P

MESH = pl.DeviceIdType.MESH
BF = jnp.bfloat16
F32 = jnp.float32
BS = 128

KEEP1 = 18
KEEP2 = 20
RAW_BOUNDS = (0, 8, 16, 24, 32, 40, 44, 46)
FIRST_BOUNDS = (46, 54, 64)
SECOND_BOUNDS = (44, 54, 64)
SIBLING_CHUNKS = 4

RIGHT, LEFT, SELF = 0, 1, 2


def nt(a, b):
    return lax.dot_general(a, b, (((1,), (1,)), ((), ())), preferred_element_type=F32)


def kernel(
    tensor, go_ref, gv_ref, partners, out,
    traw, rows, far, occ, trans, got2, perm, green, gsend, gfar, first, second,
    acc_right, acc_left, acc_self, part_right, part_left, ret_right, ret_left,
    fin_send, fin_recv, load_sem, send_sem, recv_sem,
):
    half = rows.shape[0]
    ri = rows.shape[1]
    share = ri // 2
    count = lax.axis_size("grid")
    grid_at = lax.axis_index("grid")
    core = lax.axis_index("remap")
    right = lax.rem(grid_at + 1, count)
    left = lax.rem(grid_at + count - 1, count)
    other = 1 - core

    load = pltpu.make_async_copy(tensor.at[0], traw.at[core], load_sem)
    load.start()

    barrier = pltpu.get_barrier_semaphore()
    for target in ({"grid": left}, {"grid": right}, {"remap": other}):
        pl.semaphore_signal(barrier, inc=1, device_id=target, device_id_type=MESH)

    used = [0]

    def remote(source, target, device):
        at = used[0]
        used[0] += 1
        return pltpu.make_async_remote_copy(
            src_ref=source, dst_ref=target, send_sem=send_sem.at[at], recv_sem=recv_sem.at[at],
            device_id=device, device_id_type=MESH,
        )

    to_left, to_right, to_other = {"grid": left}, {"grid": right}, {"remap": other}
    greens = remote(gsend, gfar, to_left)
    step = ri // SIBLING_CHUNKS
    siblings = [
        remote(tensor.at[0, pl.ds(i * step, step)], traw.at[core, pl.ds(i * step, step)], to_other)
        for i in range(SIBLING_CHUNKS)
    ]
    raws = [
        remote(rows.at[pl.ds(a, b - a)], far.at[pl.ds(a, b - a)], to_left)
        for a, b in zip(RAW_BOUNDS[:-1], RAW_BOUNDS[1:])
    ]
    firsts = [
        remote(trans.at[0, pl.ds(a, b - a)], first.at[pl.ds(a - FIRST_BOUNDS[0], b - a)], to_right)
        for a, b in zip(FIRST_BOUNDS[:-1], FIRST_BOUNDS[1:])
    ]
    seconds = [
        remote(trans.at[1, pl.ds(a, b - a)], second.at[pl.ds(a - SECOND_BOUNDS[0], b - a)], to_right)
        for a, b in zip(SECOND_BOUNDS[:-1], SECOND_BOUNDS[1:])
    ]
    back_right = remote(part_right, ret_right, to_left)
    back_left = remote(part_left, ret_left, to_right)
    finals = [remote(fin_send.at[d], fin_recv.at[d], to_other) for d in (RIGHT, LEFT, SELF)]

    def picked(ref, target):
        total = jnp.zeros((BS, BS), F32)
        for slot in range(2):
            weight = (partners[0, slot] == target).astype(F32)
            total = total + ref[0, slot].astype(F32) * weight
        return total.astype(BF)

    gsend[0] = picked(go_ref, left)
    gsend[1] = picked(gv_ref, left)

    out_row = lax.broadcasted_iota(jnp.int32, (256, 256), 0)
    in_row = lax.broadcasted_iota(jnp.int32, (256, 256), 1)
    perm[...] = (in_row == (out_row & 15) * 16 + (out_row >> 4)).astype(F32).astype(BF)

    pl.semaphore_wait(barrier, 3)
    greens.start()
    for copy in siblings:
        copy.start()

    n_at = lax.broadcasted_iota(jnp.int32, (half, BS), 0) + core * half
    n_of = lax.broadcasted_iota(jnp.int32, (half, BS), 1)
    choose = (n_at == n_of).astype(F32).astype(BF)
    green[pl.ds(0, half)] = nt(choose, picked(go_ref, right)).astype(BF)
    green[pl.ds(2 * half, half)] = nt(choose, picked(go_ref, grid_at)).astype(BF)
    empty = jnp.zeros((BS, BS), BF)

    def doubled(block):
        top = jnp.concatenate([block, empty], axis=1)
        bottom = jnp.concatenate([empty, block], axis=1)
        return jnp.concatenate([top, bottom], axis=0)

    got2[0] = doubled(picked(gv_ref, right))
    got2[2] = doubled(picked(gv_ref, grid_at))

    load.wait()

    def turn(n0):
        def body(i, carry):
            q0 = pl.multiple_of(i * 32, 32)
            pair = [
                traw[core, pl.ds(q0 + 16 * j, 16), pl.ds(n0, 16), :].reshape(256, BS) for j in range(2)
            ]
            turned = jnp.dot(perm[...], jnp.concatenate(pair, axis=1), preferred_element_type=F32).astype(BF)
            for j in range(2):
                rows[pl.ds(n0, 16), pl.ds(q0 + 16 * j, 16), :] = turned[:, j * BS:(j + 1) * BS].reshape(16, 16, BS)
            return carry

        lax.fori_loop(0, ri // 32, body, 0)

    sent = 0
    for n0 in range(0, half, 16):
        turn(n0)
        while sent < len(raws) and RAW_BOUNDS[sent + 1] <= n0 + 16:
            raws[sent].start()
            sent += 1

    greens.wait_recv()
    green[pl.ds(half, half)] = nt(choose, gfar[1]).astype(BF)
    got2[1] = doubled(gfar[0])

    def first_product(i, carry):
        p0 = pl.multiple_of(i * 8, 8)
        tiles = []
        for j in range(8):
            tiles.append(traw[0, p0 + j])
            tiles.append(traw[1, p0 + j])
        product = nt(green[...], jnp.concatenate(tiles, axis=0)).astype(BF)
        for j in range(8):
            occ[p0 + j] = product[:, j * BS:(j + 1) * BS]
        return carry

    for i in range(SIBLING_CHUNKS):
        siblings[i].wait_recv()
        lax.fori_loop(i * step // 8, (i + 1) * step // 8, first_product, 0)

    def second_product(direction, n0):
        def body(i, carry):
            for u in range(2):
                p0 = pl.multiple_of(i * 32 + u * 16, 16)
                pair = [
                    occ[pl.ds(p0, 16), pl.ds(direction * half + n0 + 16 * j, 16), :].reshape(256, BS)
                    for j in range(2)
                ]
                turned = jnp.dot(perm[...], jnp.concatenate(pair, axis=1), preferred_element_type=F32).astype(BF)
                product = nt(turned, got2[direction]).astype(BF)
                for j in range(2):
                    trans[direction, pl.ds(n0 + 16 * j, 16), pl.ds(p0, 16), :] = (
                        product[:, j * BS:(j + 1) * BS].reshape(16, 16, BS)
                    )
            return carry

        lax.fori_loop(0, ri // 32, body, 0)

    second_product(0, 32)
    for copy in firsts:
        copy.start()
    second_product(1, 32)
    for copy in seconds:
        copy.start()

    def wide(ref, at, many):
        return jnp.concatenate([ref[at + j] for j in range(many)], axis=1)

    def contract(acc, x, x0, y, y0, size, clear=False):
        if clear:
            acc[...] = jnp.zeros_like(acc)
        groups, rest = divmod(size, 4)

        def body(i, carry):
            acc[...] += nt(wide(x, x0 + 4 * i, 4), wide(y, y0 + 4 * i, 4))
            return carry

        if groups:
            lax.fori_loop(0, groups, body, 0)
        if rest:
            acc[...] += nt(wide(x, x0 + 4 * groups, rest), wide(y, y0 + 4 * groups, rest))

    second_product(0, 0)
    second_product(1, 0)

    def raw_chunk(i):
        a, b = RAW_BOUNDS[i], RAW_BOUNDS[i + 1]
        raws[i].wait_recv()
        contract(acc_right, trans.at[0], a, far, a, b - a, clear=i == 0)
        if b <= SECOND_BOUNDS[0]:
            contract(part_left, far, a, trans.at[1], a, b - a, clear=i == 0)

    raw_chunk(0)
    second_product(2, 32)
    second_product(2, 0)
    raw_chunk(1)
    contract(acc_self, trans.at[2], 0, rows, 0, half, clear=True)
    fin_send[SELF] = acc_self[pl.ds(pl.multiple_of(other * share, share), share), :]
    finals[SELF].start()

    raw_chunk(2)
    raw_chunk(3)
    for i, copy in enumerate(firsts):
        a, b = FIRST_BOUNDS[i], FIRST_BOUNDS[i + 1]
        copy.wait_recv()
        contract(part_right, first, a - FIRST_BOUNDS[0], rows, a, b - a, clear=i == 0)
    back_right.start()
    raw_chunk(4)
    raw_chunk(5)
    back_left.start()
    raw_chunk(6)
    for i, copy in enumerate(seconds):
        a, b = SECOND_BOUNDS[i], SECOND_BOUNDS[i + 1]
        copy.wait_recv()
        contract(acc_left, rows, a, second, a - SECOND_BOUNDS[0], b - a, clear=i == 0)

    theirs = pl.ds(pl.multiple_of(other * share, share), share)
    mine = pl.ds(pl.multiple_of(core * share, share), share)
    back_right.wait_recv()
    fin_send[RIGHT] = acc_right[theirs, :] + ret_right[theirs, :]
    finals[RIGHT].start()
    back_left.wait_recv()
    fin_send[LEFT] = acc_left[theirs, :] + ret_left[theirs, :]
    finals[LEFT].start()
    finals[SELF].wait_recv()
    out[SELF] = acc_self[mine, :] + fin_recv[SELF]
    finals[RIGHT].wait_recv()
    out[RIGHT] = acc_right[mine, :] + ret_right[mine, :] + fin_recv[RIGHT]
    finals[LEFT].wait_recv()
    out[LEFT] = acc_left[mine, :] + ret_left[mine, :] + fin_recv[LEFT]

    for copy in [greens, *siblings, *raws, *firsts, *seconds, back_right, back_left, *finals]:
        copy.wait_send()


COPIES = 1 + SIBLING_CHUNKS + len(RAW_BOUNDS) + len(FIRST_BOUNDS) + len(SECOND_BOUNDS) - 3 + 2 + 3


def on_device(tensor, go_blocks, gv_blocks, partners):
    _, ri, half, _ = tensor.shape
    share = ri // 2
    square = pltpu.VMEM((ri, ri), F32)
    vmem = pl.BlockSpec(memory_space=pltpu.VMEM)
    parts = pl.pallas_call(
        kernel,
        out_shape=jax.ShapeDtypeStruct((3, share, ri), F32),
        in_specs=[pl.BlockSpec(memory_space=pl.ANY), vmem, vmem, pl.BlockSpec(memory_space=pltpu.SMEM)],
        out_specs=vmem,
        scratch_shapes=[
            pltpu.VMEM((2, ri, half, BS), BF),
            pltpu.VMEM((half, ri, BS), BF),
            pltpu.VMEM((half - KEEP1, ri, BS), BF),
            pltpu.VMEM((ri, 3 * half, BS), BF),
            pltpu.VMEM((3, half, ri, BS), BF),
            pltpu.VMEM((3, 2 * BS, 2 * BS), BF),
            pltpu.VMEM((256, 256), BF),
            pltpu.VMEM((3 * half, BS), BF),
            pltpu.VMEM((2, BS, BS), BF),
            pltpu.VMEM((2, BS, BS), BF),
            pltpu.VMEM((KEEP1, ri, BS), BF),
            pltpu.VMEM((KEEP2, ri, BS), BF),
            square, square, square, square, square, square, square,
            pltpu.VMEM((3, share, ri), F32),
            pltpu.VMEM((3, share, ri), F32),
            pltpu.SemaphoreType.DMA,
            pltpu.SemaphoreType.DMA((COPIES,)),
            pltpu.SemaphoreType.DMA((COPIES,)),
        ],
        compiler_params=pltpu.CompilerParams(
            collective_id=0, has_side_effects=True, vmem_limit_bytes=58 * 1024 * 1024
        ),
    )(tensor, go_blocks, gv_blocks, partners)
    count = lax.axis_size("grid")
    grid_at = lax.axis_index("grid")
    where_to = partners[0][:, None, None]
    chosen = jnp.where(
        where_to == lax.rem(grid_at + 1, count),
        parts[RIGHT][None],
        jnp.where(where_to == grid_at, parts[SELF][None], parts[LEFT][None]),
    )
    return chosen[None]


def solution(mesh):
    placed = (
        P("grid", None, "remap", None),
        P("grid", None, None, None),
        P("grid", None, None, None),
        P("grid", None),
    )
    return jax.shard_map(
        on_device,
        mesh=mesh,
        in_specs=placed,
        out_specs=P("grid", None, "remap", None),
        check_vma=False,
    )
```

```python
import jax
import jax.numpy as jnp
from jax import lax
from jax.experimental import pallas as pl
from jax.experimental.pallas import tpu as pltpu
from jax.sharding import PartitionSpec as P

MESH = pl.DeviceIdType.MESH
BF = jnp.bfloat16
F32 = jnp.float32
BS = 128

KEEP1 = 20
KEEP2 = 22
RAW_BOUNDS = (0, 8, 16, 24, 32, 38, 42, 44)
FIRST_FROM = 64 - KEEP1
SECOND_BOUNDS = (42, 54, 64)
P_CHUNKS = 4

RIGHT, LEFT, SELF = 0, 1, 2


def nt(a, b):
    return lax.dot_general(a, b, (((1,), (1,)), ((), ())), preferred_element_type=F32)


def kernel(
    tensor, go_ref, gv_ref, partners, out_right, out_left, out_self,
    traw, rows, far, occ, trans, got2, perm, green, gsend, gfar, first, second,
    acc_right, acc_left, acc_self, part_right, part_left,
    back_right_send, back_left_send, ret_right, ret_left,
    fin_send, fin_recv, load_sem, send_sem, recv_sem,
):
    half = rows.shape[0]
    ri = rows.shape[1]
    share = ri // 2
    count = lax.axis_size("grid")
    grid_at = lax.axis_index("grid")
    core = lax.axis_index("remap")
    right = lax.rem(grid_at + 1, count)
    left = lax.rem(grid_at + count - 1, count)
    other = 1 - core

    def loaded(at, n0, size):
        span = pl.ds(n0, size)
        return pltpu.make_async_copy(tensor.at[0, :, span], traw.at[core, :, span], load_sem.at[at])

    loads = [loaded(0, 0, 16), loaded(1, 16, half - 16)]
    for copy in loads:
        copy.start()

    barrier = pltpu.get_barrier_semaphore()
    for target in ({"grid": left}, {"grid": right}, {"remap": other}):
        pl.semaphore_signal(barrier, inc=1, device_id=target, device_id_type=MESH)

    used = [0]

    def remote(source, target, device):
        at = used[0]
        used[0] += 1
        return pltpu.make_async_remote_copy(
            src_ref=source, dst_ref=target, send_sem=send_sem.at[at], recv_sem=recv_sem.at[at],
            device_id=device, device_id_type=MESH,
        )

    to_left, to_right, to_other = {"grid": left}, {"grid": right}, {"remap": other}
    greens = remote(gsend, gfar, to_left)
    step = ri // P_CHUNKS
    siblings = [
        remote(tensor.at[0, pl.ds(i * step, step)], traw.at[core, pl.ds(i * step, step)], to_other)
        for i in range(P_CHUNKS)
    ]
    raws = [
        remote(rows.at[pl.ds(a, b - a)], far.at[pl.ds(a, b - a)], to_left)
        for a, b in zip(RAW_BOUNDS[:-1], RAW_BOUNDS[1:])
    ]
    firsts = [
        remote(
            trans.at[0, pl.ds(FIRST_FROM, KEEP1), pl.ds(i * step, step)],
            first.at[:, pl.ds(i * step, step)],
            to_right,
        )
        for i in range(P_CHUNKS)
    ]
    seconds = [
        remote(trans.at[1, pl.ds(a, b - a)], second.at[pl.ds(a - SECOND_BOUNDS[0], b - a)], to_right)
        for a, b in zip(SECOND_BOUNDS[:-1], SECOND_BOUNDS[1:])
    ]
    back_right = remote(back_right_send, ret_right, to_left)
    back_left = remote(back_left_send, ret_left, to_right)
    finals = [remote(fin_send.at[d], fin_recv.at[d], to_other) for d in (RIGHT, LEFT, SELF)]

    def picked(ref, target):
        total = jnp.zeros((BS, BS), F32)
        for slot in range(2):
            weight = (partners[0, slot] == target).astype(F32)
            total = total + ref[0, slot].astype(F32) * weight
        return total.astype(BF)

    gsend[0] = picked(go_ref, left)
    gsend[1] = picked(gv_ref, left)

    out_row = lax.broadcasted_iota(jnp.int32, (256, 256), 0)
    in_row = lax.broadcasted_iota(jnp.int32, (256, 256), 1)
    perm[...] = (in_row == (out_row & 15) * 16 + (out_row >> 4)).astype(F32).astype(BF)

    n_at = lax.broadcasted_iota(jnp.int32, (half, BS), 0) + core * half
    n_of = lax.broadcasted_iota(jnp.int32, (half, BS), 1)
    choose = (n_at == n_of).astype(F32).astype(BF)
    green[pl.ds(0, half)] = nt(choose, picked(go_ref, right)).astype(BF)
    green[pl.ds(2 * half, half)] = nt(choose, picked(go_ref, grid_at)).astype(BF)
    empty = jnp.zeros((BS, BS), BF)

    def doubled(block):
        top = jnp.concatenate([block, empty], axis=1)
        bottom = jnp.concatenate([empty, block], axis=1)
        return jnp.concatenate([top, bottom], axis=0)

    got2[0] = doubled(picked(gv_ref, right))
    got2[2] = doubled(picked(gv_ref, grid_at))

    def turn(n0):
        def body(i, carry):
            q0 = pl.multiple_of(i * 32, 32)
            pair = [
                traw[core, pl.ds(q0 + 16 * j, 16), pl.ds(n0, 16), :].reshape(256, BS) for j in range(2)
            ]
            turned = jnp.dot(perm[...], jnp.concatenate(pair, axis=1), preferred_element_type=F32).astype(BF)
            for j in range(2):
                rows[pl.ds(n0, 16), pl.ds(q0 + 16 * j, 16), :] = turned[:, j * BS:(j + 1) * BS].reshape(16, 16, BS)
            return carry

        lax.fori_loop(0, ri // 32, body, 0)

    loads[0].wait()
    turn(0)

    pl.semaphore_wait(barrier, 3)
    greens.start()
    for copy in siblings:
        copy.start()
    raws[0].start()
    raws[1].start()
    loads[1].wait()

    greens.wait_recv()
    green[pl.ds(half, half)] = nt(choose, gfar[1]).astype(BF)
    got2[1] = doubled(gfar[0])

    def first_product(i, carry):
        p0 = pl.multiple_of(i * 8, 8)
        tiles = []
        for j in range(8):
            tiles.append(traw[0, p0 + j])
            tiles.append(traw[1, p0 + j])
        product = nt(green[...], jnp.concatenate(tiles, axis=0)).astype(BF)
        for j in range(8):
            occ[p0 + j] = product[:, j * BS:(j + 1) * BS]
        return carry

    def second_product(direction, n0, start, size):
        def body(i, carry):
            for u in range(2):
                p0 = pl.multiple_of(i * 32 + u * 16, 16)
                pair = [
                    occ[pl.ds(p0, 16), pl.ds(direction * half + n0 + 16 * j, 16), :].reshape(256, BS)
                    for j in range(2)
                ]
                turned = jnp.dot(perm[...], jnp.concatenate(pair, axis=1), preferred_element_type=F32).astype(BF)
                product = nt(turned, got2[direction]).astype(BF)
                for j in range(2):
                    trans[direction, pl.ds(n0 + 16 * j, 16), pl.ds(p0, 16), :] = (
                        product[:, j * BS:(j + 1) * BS].reshape(16, 16, BS)
                    )
            return carry

        lax.fori_loop(start // 32, (start + size) // 32, body, 0)

    for i in range(P_CHUNKS):
        siblings[i].wait_recv()
        lax.fori_loop(i * step // 8, (i + 1) * step // 8, first_product, 0)
        second_product(0, 32, i * step, step)
        firsts[i].start()
    turn(16)
    raws[2].start()
    second_product(1, 32, 0, ri)
    seconds[0].start()
    turn(32)
    turn(48)

    def wide(ref, at, many):
        return jnp.concatenate([ref[at + j] for j in range(many)], axis=1)

    def contract(acc, x, x0, y, y0, size, clear=False):
        if clear:
            acc[...] = jnp.zeros_like(acc)
        groups, rest = divmod(size, 4)

        def body(i, carry):
            acc[...] += nt(wide(x, x0 + 4 * i, 4), wide(y, y0 + 4 * i, 4))
            return carry

        if groups:
            lax.fori_loop(0, groups, body, 0)
        if rest:
            acc[...] += nt(wide(x, x0 + 4 * groups, rest), wide(y, y0 + 4 * groups, rest))

    second_product(0, 0, 0, ri)
    second_product(1, 0, 0, ri)

    theirs = pl.ds(pl.multiple_of(other * share, share), share)
    mine = pl.ds(pl.multiple_of(core * share, share), share)

    def raw_chunk(i):
        a, b = RAW_BOUNDS[i], RAW_BOUNDS[i + 1]
        raws[i].wait_recv()
        if i + 3 < len(raws):
            raws[i + 3].start()
        contract(acc_right, trans.at[0], a, far, a, b - a, clear=i == 0)
        if b <= SECOND_BOUNDS[0]:
            contract(part_left, far, a, trans.at[1], a, b - a, clear=i == 0)

    def second_chunk(i):
        a, b = SECOND_BOUNDS[i], SECOND_BOUNDS[i + 1]
        seconds[i].wait_recv()
        contract(acc_left, rows, a, second, a - SECOND_BOUNDS[0], b - a, clear=i == 0)

    raw_chunk(0)
    second_product(2, 32, 0, ri)
    second_product(2, 0, 0, ri)
    raw_chunk(1)
    contract(acc_self, trans.at[2], 0, rows, 0, half, clear=True)
    fin_send[SELF] = acc_self[theirs, :]
    finals[SELF].start()

    raw_chunk(2)
    for copy in firsts:
        copy.wait_recv()
    seconds[1].start()
    contract(part_right, first, 0, rows, FIRST_FROM, KEEP1, clear=True)
    back_right_send[...] = part_right[...].astype(BF)
    back_right.start()
    finals[SELF].wait_recv()
    out_self[...] = acc_self[mine, :] + fin_recv[SELF]
    raw_chunk(3)
    raw_chunk(4)
    second_chunk(0)
    raw_chunk(5)
    back_left_send[...] = part_left[...].astype(BF)
    back_left.start()
    raw_chunk(6)

    back_right.wait_recv()
    fin_send[RIGHT] = acc_right[theirs, :] + ret_right[theirs, :].astype(F32)
    finals[RIGHT].start()
    second_chunk(1)
    back_left.wait_recv()
    fin_send[LEFT] = acc_left[theirs, :] + ret_left[theirs, :].astype(F32)
    finals[LEFT].start()
    finals[RIGHT].wait_recv()
    out_right[...] = acc_right[mine, :] + ret_right[mine, :].astype(F32) + fin_recv[RIGHT]
    finals[LEFT].wait_recv()
    out_left[...] = acc_left[mine, :] + ret_left[mine, :].astype(F32) + fin_recv[LEFT]

    for copy in [greens, *siblings, *raws, *firsts, *seconds, back_right, back_left, *finals]:
        copy.wait_send()


COPIES = 1 + 2 * P_CHUNKS + len(RAW_BOUNDS) + len(SECOND_BOUNDS) - 2 + 2 + 3


def on_device(tensor, go_blocks, gv_blocks, partners):
    _, ri, half, _ = tensor.shape
    share = ri // 2
    square = pltpu.VMEM((ri, ri), F32)
    narrow = pltpu.VMEM((ri, ri), BF)
    vmem = pl.BlockSpec(memory_space=pltpu.VMEM)
    result = jax.ShapeDtypeStruct((share, ri), F32)
    to_right, to_left, to_self = pl.pallas_call(
        kernel,
        out_shape=[result] * 3,
        in_specs=[pl.BlockSpec(memory_space=pl.ANY), vmem, vmem, pl.BlockSpec(memory_space=pltpu.SMEM)],
        out_specs=[vmem] * 3,
        scratch_shapes=[
            pltpu.VMEM((2, ri, half, BS), BF),
            pltpu.VMEM((half, ri, BS), BF),
            pltpu.VMEM((half - KEEP1, ri, BS), BF),
            pltpu.VMEM((ri, 3 * half, BS), BF),
            pltpu.VMEM((3, half, ri, BS), BF),
            pltpu.VMEM((3, 2 * BS, 2 * BS), BF),
            pltpu.VMEM((256, 256), BF),
            pltpu.VMEM((3 * half, BS), BF),
            pltpu.VMEM((2, BS, BS), BF),
            pltpu.VMEM((2, BS, BS), BF),
            pltpu.VMEM((KEEP1, ri, BS), BF),
            pltpu.VMEM((KEEP2, ri, BS), BF),
            square, square, square, square, square,
            narrow, narrow, narrow, narrow,
            pltpu.VMEM((3, share, ri), F32),
            pltpu.VMEM((3, share, ri), F32),
            pltpu.SemaphoreType.DMA((2,)),
            pltpu.SemaphoreType.DMA((COPIES,)),
            pltpu.SemaphoreType.DMA((COPIES,)),
        ],
        compiler_params=pltpu.CompilerParams(
            collective_id=0, has_side_effects=True, vmem_limit_bytes=58 * 1024 * 1024
        ),
    )(tensor, go_blocks, gv_blocks, partners)
    count = lax.axis_size("grid")
    grid_at = lax.axis_index("grid")
    where_to = partners[0][:, None, None]
    chosen = jnp.where(
        where_to == lax.rem(grid_at + 1, count),
        to_right[None],
        jnp.where(where_to == grid_at, to_self[None], to_left[None]),
    )
    return chosen[None]


def solution(mesh):
    placed = (
        P("grid", None, "remap", None),
        P("grid", None, None, None),
        P("grid", None, None, None),
        P("grid", None),
    )
    return jax.shard_map(
        on_device,
        mesh=mesh,
        in_specs=placed,
        out_specs=P("grid", None, "remap", None),
        check_vma=False,
    )
```

```python
import jax
import jax.numpy as jnp
from jax import lax
from jax.experimental import pallas as pl
from jax.experimental.pallas import tpu as pltpu
from jax.sharding import PartitionSpec as P

MESH = pl.DeviceIdType.MESH
BF = jnp.bfloat16
F32 = jnp.float32
BS = 128

KEEP1 = 20
KEEP2 = 23
RAW_BOUNDS = (0, 8, 16, 24, 32, 37, 41, 44)
FIRST_FROM = 64 - KEEP1
SECOND_BOUNDS = (41, 53, 64)
P_BOUNDS = (0, 32, 64, 128, 256)
P_CHUNKS = len(P_BOUNDS) - 1

RIGHT, LEFT, SELF = 0, 1, 2


def nt(a, b):
    return lax.dot_general(a, b, (((1,), (1,)), ((), ())), preferred_element_type=F32)


def kernel(
    tensor, go_hbm, gv_hbm, partners, out,
    traw, rows, far, occ, trans, got2, perm, green, go_ref, gv_ref, gsend, gfar, first, second,
    acc_right, acc_left, acc_self, part_right, part_left,
    half_send, half_recv, back_right_send, back_left_send, ret_right, ret_left,
    fin_send, fin_recv, load_sem, send_sem, recv_sem,
):
    half = rows.shape[0]
    ri = rows.shape[1]
    share = ri // 2
    count = lax.axis_size("grid")
    grid_at = lax.axis_index("grid")
    core = lax.axis_index("remap")
    right = lax.rem(grid_at + 1, count)
    left = lax.rem(grid_at + count - 1, count)
    other = 1 - core

    barrier = pltpu.get_barrier_semaphore()
    for target in ({"grid": left}, {"grid": right}, {"remap": other}):
        pl.semaphore_signal(barrier, inc=1, device_id=target, device_id_type=MESH)

    def loaded(at, n0, size):
        span = pl.ds(n0, size)
        return pltpu.make_async_copy(tensor.at[0, :, span], traw.at[core, :, span], load_sem.at[at])

    loads = [loaded(0, 0, 16), loaded(1, 16, half - 16)]
    loads += [
        pltpu.make_async_copy(go_hbm.at[0], go_ref, load_sem.at[2]),
        pltpu.make_async_copy(gv_hbm.at[0], gv_ref, load_sem.at[3]),
    ]
    for copy in loads[2:] + loads[:2]:
        copy.start()

    used = [0]

    def remote(source, target, device):
        at = used[0]
        used[0] += 1
        return pltpu.make_async_remote_copy(
            src_ref=source, dst_ref=target, send_sem=send_sem.at[at], recv_sem=recv_sem.at[at],
            device_id=device, device_id_type=MESH,
        )

    to_left, to_right, to_other = {"grid": left}, {"grid": right}, {"remap": other}
    greens = remote(gsend, gfar, to_left)
    theirs = pl.ds(pl.multiple_of(other * share, share), share)
    mine = pl.ds(pl.multiple_of(core * share, share), share)
    p_spans = [pl.ds(a, b - a) for a, b in zip(P_BOUNDS[:-1], P_BOUNDS[1:])]
    siblings = [
        remote(tensor.at[0, span], traw.at[core, span], to_other)
        for span in p_spans
    ]
    raws = [
        remote(rows.at[pl.ds(a, b - a)], far.at[pl.ds(a, b - a)], to_left)
        for a, b in zip(RAW_BOUNDS[:-1], RAW_BOUNDS[1:])
    ]
    firsts = [
        remote(trans.at[0, pl.ds(FIRST_FROM, KEEP1), span], first.at[:, span], to_right)
        for span in p_spans
    ]
    seconds = [
        remote(trans.at[1, pl.ds(a, b - a)], second.at[pl.ds(a - SECOND_BOUNDS[0], b - a)], to_right)
        for a, b in zip(SECOND_BOUNDS[:-1], SECOND_BOUNDS[1:])
    ]
    back_right = remote(back_right_send, ret_right, to_left)
    back_left = remote(back_left_send, ret_left, to_right)
    halves = [remote(half_send.at[d], half_recv.at[d], to_other) for d in (RIGHT, LEFT)]
    finals = [remote(fin_send.at[d], fin_recv.at[d], to_other) for d in (RIGHT, LEFT, SELF)]

    def picked(ref, target):
        total = jnp.zeros((BS, BS), F32)
        for slot in range(2):
            weight = (partners[0, slot] == target).astype(F32)
            total = total + ref[slot].astype(F32) * weight
        return total.astype(BF)

    out_row = lax.broadcasted_iota(jnp.int32, (256, 256), 0)
    in_row = lax.broadcasted_iota(jnp.int32, (256, 256), 1)
    perm[...] = (in_row == (out_row & 15) * 16 + (out_row >> 4)).astype(F32).astype(BF)

    n_at = lax.broadcasted_iota(jnp.int32, (half, BS), 0) + core * half
    n_of = lax.broadcasted_iota(jnp.int32, (half, BS), 1)
    choose = (n_at == n_of).astype(F32).astype(BF)
    loads[2].wait()
    loads[3].wait()
    gsend[pl.ds(0, BS)] = picked(go_ref, left)
    gsend[pl.ds(BS, half)] = nt(choose, picked(gv_ref, left)).astype(BF)
    green[pl.ds(0, half)] = nt(choose, picked(go_ref, right)).astype(BF)
    green[pl.ds(2 * half, half)] = nt(choose, picked(go_ref, grid_at)).astype(BF)
    empty = jnp.zeros((BS, BS), BF)

    def doubled(block):
        top = jnp.concatenate([block, empty], axis=1)
        bottom = jnp.concatenate([empty, block], axis=1)
        return jnp.concatenate([top, bottom], axis=0)

    got2[0] = doubled(picked(gv_ref, right))
    got2[2] = doubled(picked(gv_ref, grid_at))

    def turn(n0):
        def body(i, carry):
            q0 = pl.multiple_of(i * 32, 32)
            pair = [
                traw[core, pl.ds(q0 + 16 * j, 16), pl.ds(n0, 16), :].reshape(256, BS) for j in range(2)
            ]
            turned = jnp.dot(perm[...], jnp.concatenate(pair, axis=1), preferred_element_type=F32).astype(BF)
            for j in range(2):
                rows[pl.ds(n0, 16), pl.ds(q0 + 16 * j, 16), :] = turned[:, j * BS:(j + 1) * BS].reshape(16, 16, BS)
            return carry

        lax.fori_loop(0, ri // 32, body, 0)

    loads[0].wait()
    turn(0)

    pl.semaphore_wait(barrier, 3)
    greens.start()
    for copy in siblings:
        copy.start()
    raws[0].start()
    raws[1].start()
    loads[1].wait()

    greens.wait_recv()
    green[pl.ds(half, half)] = gfar[pl.ds(BS, half)]
    got2[1] = doubled(gfar[pl.ds(0, BS)])

    def first_product(i, carry):
        p0 = pl.multiple_of(i * 8, 8)
        tiles = []
        for j in range(8):
            tiles.append(traw[0, p0 + j])
            tiles.append(traw[1, p0 + j])
        product = nt(green[...], jnp.concatenate(tiles, axis=0)).astype(BF)
        for j in range(8):
            occ[p0 + j] = product[:, j * BS:(j + 1) * BS]
        return carry

    def second_product(direction, n0, start, size):
        def body(i, carry):
            for u in range(2):
                p0 = pl.multiple_of(i * 32 + u * 16, 16)
                pair = [
                    occ[pl.ds(p0, 16), pl.ds(direction * half + n0 + 16 * j, 16), :].reshape(256, BS)
                    for j in range(2)
                ]
                turned = jnp.dot(perm[...], jnp.concatenate(pair, axis=1), preferred_element_type=F32).astype(BF)
                product = nt(turned, got2[direction]).astype(BF)
                for j in range(2):
                    trans[direction, pl.ds(n0 + 16 * j, 16), pl.ds(p0, 16), :] = (
                        product[:, j * BS:(j + 1) * BS].reshape(16, 16, BS)
                    )
            return carry

        lax.fori_loop(start // 32, (start + size) // 32, body, 0)

    for i in range(P_CHUNKS):
        siblings[i].wait_recv()
        a, b = P_BOUNDS[i], P_BOUNDS[i + 1]
        lax.fori_loop(a // 8, b // 8, first_product, 0)
        second_product(0, 32, a, b - a)
        firsts[i].start()
    turn(16)
    raws[2].start()
    second_product(1, 32, 0, ri)
    seconds[0].start()
    turn(32)
    turn(48)

    def wide(ref, at, many):
        return jnp.concatenate([ref[at + j] for j in range(many)], axis=1)

    def contract(acc, x, x0, y, y0, size, clear=False):
        if clear:
            acc[...] = jnp.zeros_like(acc)
        groups, rest = divmod(size, 4)

        def body(i, carry):
            acc[...] += nt(wide(x, x0 + 4 * i, 4), wide(y, y0 + 4 * i, 4))
            return carry

        if groups:
            lax.fori_loop(0, groups, body, 0)
        if rest:
            acc[...] += nt(wide(x, x0 + 4 * groups, rest), wide(y, y0 + 4 * groups, rest))

    second_product(0, 0, 0, ri)
    second_product(1, 0, 0, ri)

    def swap_halves(direction, part):
        half_send[direction] = part[theirs, :]
        halves[direction].start()

    def send_back(direction, part, narrow, copy):
        halves[direction].wait_recv()
        narrow[...] = (part[mine, :] + half_recv[direction]).astype(BF)
        copy.start()

    def put(target, total, clear=False):
        for slot in range(2):
            term = total * (partners[0, slot] == target).astype(F32)
            out[slot] = term if clear else out[slot] + term

    def raw_chunk(i):
        a, b = RAW_BOUNDS[i], RAW_BOUNDS[i + 1]
        raws[i].wait_recv()
        if i + 3 < len(raws):
            raws[i + 3].start()
        contract(acc_right, trans.at[0], a, far, a, b - a, clear=i == 0)
        if b <= SECOND_BOUNDS[0]:
            contract(part_left, far, a, trans.at[1], a, b - a, clear=i == 0)

    def second_chunk(i):
        a, b = SECOND_BOUNDS[i], SECOND_BOUNDS[i + 1]
        seconds[i].wait_recv()
        contract(acc_left, rows, a, second, a - SECOND_BOUNDS[0], b - a, clear=i == 0)

    raw_chunk(0)
    second_product(2, 32, 0, ri)
    second_product(2, 0, 0, ri)
    raw_chunk(1)
    contract(acc_self, trans.at[2], 0, rows, 0, half, clear=True)
    fin_send[SELF] = acc_self[theirs, :]
    finals[SELF].start()

    raw_chunk(2)
    for copy in firsts:
        copy.wait_recv()
    seconds[1].start()
    contract(part_right, first, 0, rows, FIRST_FROM, KEEP1, clear=True)
    swap_halves(RIGHT, part_right)
    finals[SELF].wait_recv()
    put(grid_at, acc_self[mine, :] + fin_recv[SELF], clear=True)
    send_back(RIGHT, part_right, back_right_send, back_right)
    raw_chunk(3)
    raw_chunk(4)
    second_chunk(0)
    raw_chunk(5)
    swap_halves(LEFT, part_left)
    send_back(LEFT, part_left, back_left_send, back_left)
    raw_chunk(6)

    fin_send[RIGHT] = acc_right[theirs, :]
    finals[RIGHT].start()
    second_chunk(1)
    fin_send[LEFT] = acc_left[theirs, :]
    finals[LEFT].start()
    back_right.wait_recv()
    finals[RIGHT].wait_recv()
    put(right, acc_right[mine, :] + ret_right[...].astype(F32) + fin_recv[RIGHT])
    back_left.wait_recv()
    finals[LEFT].wait_recv()
    put(left, acc_left[mine, :] + ret_left[...].astype(F32) + fin_recv[LEFT])

    for copy in [greens, *siblings, *raws, *firsts, *seconds, *halves, back_right, back_left, *finals]:
        copy.wait_send()


COPIES = 1 + 2 * P_CHUNKS + len(RAW_BOUNDS) + len(SECOND_BOUNDS) - 2 + 4 + 3


def on_device(tensor, go_blocks, gv_blocks, partners):
    _, ri, half, _ = tensor.shape
    share = ri // 2
    square = pltpu.VMEM((ri, ri), F32)
    narrow = pltpu.VMEM((share, ri), BF)
    blocks = pltpu.VMEM((2, BS, BS), BF)
    green_rows = pltpu.VMEM((BS + half, BS), BF)
    result = pl.pallas_call(
        kernel,
        out_shape=jax.ShapeDtypeStruct((2, share, ri), F32),
        in_specs=[pl.BlockSpec(memory_space=pl.ANY)] * 3 + [pl.BlockSpec(memory_space=pltpu.SMEM)],
        out_specs=pl.BlockSpec(memory_space=pltpu.VMEM),
        scratch_shapes=[
            pltpu.VMEM((2, ri, half, BS), BF),
            pltpu.VMEM((half, ri, BS), BF),
            pltpu.VMEM((half - KEEP1, ri, BS), BF),
            pltpu.VMEM((ri, 3 * half, BS), BF),
            pltpu.VMEM((3, half, ri, BS), BF),
            pltpu.VMEM((3, 2 * BS, 2 * BS), BF),
            pltpu.VMEM((256, 256), BF),
            pltpu.VMEM((3 * half, BS), BF),
            blocks, blocks, green_rows, green_rows,
            pltpu.VMEM((KEEP1, ri, BS), BF),
            pltpu.VMEM((KEEP2, ri, BS), BF),
            square, square, square, square, square,
            pltpu.VMEM((2, share, ri), F32),
            pltpu.VMEM((2, share, ri), F32),
            narrow, narrow, narrow, narrow,
            pltpu.VMEM((3, share, ri), F32),
            pltpu.VMEM((3, share, ri), F32),
            pltpu.SemaphoreType.DMA((4,)),
            pltpu.SemaphoreType.DMA((COPIES,)),
            pltpu.SemaphoreType.DMA((COPIES,)),
        ],
        compiler_params=pltpu.CompilerParams(
            collective_id=0, has_side_effects=True, vmem_limit_bytes=58 * 1024 * 1024
        ),
    )(tensor, go_blocks, gv_blocks, partners)
    return result[None]


def solution(mesh):
    placed = (
        P("grid", None, "remap", None),
        P("grid", None, None, None),
        P("grid", None, None, None),
        P("grid", None),
    )
    return jax.shard_map(
        on_device,
        mesh=mesh,
        in_specs=placed,
        out_specs=P("grid", None, "remap", None),
        check_vma=False,
    )
```

```python
import jax
import jax.numpy as jnp
from jax import lax
from jax.experimental import pallas as pl
from jax.experimental.pallas import tpu as pltpu
from jax.sharding import PartitionSpec as P

MESH = pl.DeviceIdType.MESH
BF = jnp.bfloat16
F32 = jnp.float32
BS = 128

KEEP1 = 20
KEEP2 = 23
RAW_BOUNDS = (0, 8, 16, 24, 32, 37, 41, 44)
FIRST_FROM = 64 - KEEP1
SECOND_BOUNDS = (41, 51, 59, 64)
P_BOUNDS = (0, 32, 64, 128, 256)
P_CHUNKS = len(P_BOUNDS) - 1

RIGHT, LEFT, SELF = 0, 1, 2


def nt(a, b):
    return lax.dot_general(a, b, (((1,), (1,)), ((), ())), preferred_element_type=F32)


def kernel(
    tensor, go_hbm, gv_hbm, partners, out,
    traw, rows, far, occ, trans, got2, perm, green, go_ref, gv_ref, gsend, gfar, first, second,
    acc_right, acc_left, acc_self, part_right, part_left,
    half_send, half_recv, back_right_send, back_left_send, ret_right, ret_left,
    fin_send, fin_recv, load_sem, send_sem, recv_sem,
):
    half = rows.shape[0]
    ri = rows.shape[1]
    share = ri // 2
    count = lax.axis_size("grid")
    grid_at = lax.axis_index("grid")
    core = lax.axis_index("remap")
    right = lax.rem(grid_at + 1, count)
    left = lax.rem(grid_at + count - 1, count)
    other = 1 - core

    barrier = pltpu.get_barrier_semaphore()
    for target in ({"grid": left}, {"grid": right}, {"remap": other}):
        pl.semaphore_signal(barrier, inc=1, device_id=target, device_id_type=MESH)

    def loaded(at, n0, size):
        span = pl.ds(n0, size)
        return pltpu.make_async_copy(tensor.at[0, :, span], traw.at[core, :, span], load_sem.at[at])

    loads = [loaded(0, 0, 16), loaded(1, 16, half - 16)]
    loads += [
        pltpu.make_async_copy(go_hbm.at[0], go_ref, load_sem.at[2]),
        pltpu.make_async_copy(gv_hbm.at[0], gv_ref, load_sem.at[3]),
    ]
    for copy in loads[2:] + loads[:2]:
        copy.start()

    used = [0]

    def remote(source, target, device):
        at = used[0]
        used[0] += 1
        return pltpu.make_async_remote_copy(
            src_ref=source, dst_ref=target, send_sem=send_sem.at[at], recv_sem=recv_sem.at[at],
            device_id=device, device_id_type=MESH,
        )

    to_left, to_right, to_other = {"grid": left}, {"grid": right}, {"remap": other}
    greens = remote(gsend, gfar, to_left)
    theirs = pl.ds(pl.multiple_of(other * share, share), share)
    mine = pl.ds(pl.multiple_of(core * share, share), share)
    p_spans = [pl.ds(a, b - a) for a, b in zip(P_BOUNDS[:-1], P_BOUNDS[1:])]
    siblings = [
        remote(tensor.at[0, span], traw.at[core, span], to_other)
        for span in p_spans
    ]
    raws = [
        remote(rows.at[pl.ds(a, b - a)], far.at[pl.ds(a, b - a)], to_left)
        for a, b in zip(RAW_BOUNDS[:-1], RAW_BOUNDS[1:])
    ]
    firsts = [
        remote(trans.at[0, pl.ds(FIRST_FROM, KEEP1), span], first.at[:, span], to_right)
        for span in p_spans
    ]
    seconds = [
        remote(trans.at[1, pl.ds(a, b - a)], second.at[pl.ds(a - SECOND_BOUNDS[0], b - a)], to_right)
        for a, b in zip(SECOND_BOUNDS[:-1], SECOND_BOUNDS[1:])
    ]
    back_right = remote(back_right_send, ret_right, to_left)
    back_left = remote(back_left_send, ret_left, to_right)
    halves = [remote(half_send.at[d], half_recv.at[d], to_other) for d in (RIGHT, LEFT)]
    finals = [remote(fin_send.at[d], fin_recv.at[d], to_other) for d in (RIGHT, LEFT, SELF)]

    def picked(ref, target):
        total = jnp.zeros((BS, BS), F32)
        for slot in range(2):
            weight = (partners[0, slot] == target).astype(F32)
            total = total + ref[slot].astype(F32) * weight
        return total.astype(BF)

    out_row = lax.broadcasted_iota(jnp.int32, (256, 256), 0)
    in_row = lax.broadcasted_iota(jnp.int32, (256, 256), 1)
    perm[...] = (in_row == (out_row & 15) * 16 + (out_row >> 4)).astype(F32).astype(BF)

    n_at = lax.broadcasted_iota(jnp.int32, (half, BS), 0) + core * half
    n_of = lax.broadcasted_iota(jnp.int32, (half, BS), 1)
    choose = (n_at == n_of).astype(F32).astype(BF)
    loads[2].wait()
    loads[3].wait()
    gsend[pl.ds(0, BS)] = picked(go_ref, left)
    gsend[pl.ds(BS, half)] = nt(choose, picked(gv_ref, left)).astype(BF)
    green[pl.ds(0, half)] = nt(choose, picked(go_ref, right)).astype(BF)
    green[pl.ds(2 * half, half)] = nt(choose, picked(go_ref, grid_at)).astype(BF)
    empty = jnp.zeros((BS, BS), BF)

    def doubled(block):
        top = jnp.concatenate([block, empty], axis=1)
        bottom = jnp.concatenate([empty, block], axis=1)
        return jnp.concatenate([top, bottom], axis=0)

    got2[0] = doubled(picked(gv_ref, right))
    got2[2] = doubled(picked(gv_ref, grid_at))

    def turn(n_blocks):
        width = 64 if len(n_blocks) == 1 else 32

        def body(i, carry):
            for n0 in n_blocks:
                for u in range(width // 32):
                    q0 = pl.multiple_of(i * width + u * 32, 32)
                    pair = [
                        traw[core, pl.ds(q0 + 16 * j, 16), pl.ds(n0, 16), :].reshape(256, BS) for j in range(2)
                    ]
                    turned = jnp.dot(
                        perm[...], jnp.concatenate(pair, axis=1), preferred_element_type=F32
                    ).astype(BF)
                    for j in range(2):
                        rows[pl.ds(n0, 16), pl.ds(q0 + 16 * j, 16), :] = (
                            turned[:, j * BS:(j + 1) * BS].reshape(16, 16, BS)
                        )
            return carry

        lax.fori_loop(0, ri // width, body, 0)

    loads[0].wait()
    turn([0])

    pl.semaphore_wait(barrier, 3)
    greens.start()
    for copy in siblings:
        copy.start()
    raws[0].start()
    raws[1].start()
    loads[1].wait()

    greens.wait_recv()
    green[pl.ds(half, half)] = gfar[pl.ds(BS, half)]
    got2[1] = doubled(gfar[pl.ds(0, BS)])

    def first_product(i, carry):
        p0 = pl.multiple_of(i * 8, 8)
        tiles = []
        for j in range(8):
            tiles.append(traw[0, p0 + j])
            tiles.append(traw[1, p0 + j])
        product = nt(green[...], jnp.concatenate(tiles, axis=0)).astype(BF)
        for j in range(8):
            occ[p0 + j] = product[:, j * BS:(j + 1) * BS]
        return carry

    def second_product(parts, start, size):
        width = 32 if len(parts) > 1 or size == 32 else 64

        def body(i, carry):
            for direction, n0 in parts:
                for u in range(width // 16):
                    p0 = pl.multiple_of(i * width + u * 16, 16)
                    pair = [
                        occ[pl.ds(p0, 16), pl.ds(direction * half + n0 + 16 * j, 16), :].reshape(256, BS)
                        for j in range(2)
                    ]
                    turned = jnp.dot(
                        perm[...], jnp.concatenate(pair, axis=1), preferred_element_type=F32
                    ).astype(BF)
                    product = nt(turned, got2[direction]).astype(BF)
                    for j in range(2):
                        trans[direction, pl.ds(n0 + 16 * j, 16), pl.ds(p0, 16), :] = (
                            product[:, j * BS:(j + 1) * BS].reshape(16, 16, BS)
                        )
            return carry

        lax.fori_loop(start // width, (start + size) // width, body, 0)

    for i in range(P_CHUNKS):
        siblings[i].wait_recv()
        a, b = P_BOUNDS[i], P_BOUNDS[i + 1]
        lax.fori_loop(a // 8, b // 8, first_product, 0)
        second_product([(0, 32)], a, b - a)
        firsts[i].start()
    turn([16])
    raws[2].start()
    second_product([(1, 32)], 0, ri)
    seconds[0].start()
    turn([32, 48])
    raws[3].start()
    raws[4].start()

    def wide(ref, at, many):
        return jnp.concatenate([ref[at + j] for j in range(many)], axis=1)

    def contract(jobs, size, clear=False):
        if clear:
            for acc, *_ in jobs:
                acc[...] = jnp.zeros_like(acc)
        groups, rest = divmod(size, 8)

        def add(at, many):
            for acc, x, x0, y, y0 in jobs:
                acc[...] += nt(wide(x, x0 + at, many), wide(y, y0 + at, many))

        def body(i, carry):
            add(8 * i, 8)
            return carry

        if groups > 1:
            lax.fori_loop(0, groups, body, 0)
        elif groups:
            add(0, 8)
        if rest:
            add(8 * groups, rest)

    second_product([(0, 0), (1, 0)], 0, ri)

    def swap_halves(direction, part):
        half_send[direction] = part[theirs, :]
        halves[direction].start()

    def send_back(direction, part, narrow, copy):
        halves[direction].wait_recv()
        narrow[...] = (part[mine, :] + half_recv[direction]).astype(BF)
        copy.start()

    def put(target, total, clear=False):
        for slot in range(2):
            term = total * (partners[0, slot] == target).astype(F32)
            out[slot] = term if clear else out[slot] + term

    def raw_chunk(i):
        a, b = RAW_BOUNDS[i], RAW_BOUNDS[i + 1]
        raws[i].wait_recv()
        jobs = [(acc_right, trans.at[0], a, far, a)]
        if b <= SECOND_BOUNDS[0]:
            jobs.append((part_left, far, a, trans.at[1], a))
        contract(jobs, b - a, clear=i == 0)

    def second_chunk(i):
        a, b = SECOND_BOUNDS[i], SECOND_BOUNDS[i + 1]
        seconds[i].wait_recv()
        contract([(acc_left, rows, a, second, a - SECOND_BOUNDS[0])], b - a, clear=i == 0)

    raw_chunk(0)
    raws[5].start()
    seconds[1].start()
    second_product([(2, 32), (2, 0)], 0, ri)
    raw_chunk(1)
    raws[6].start()
    seconds[2].start()
    contract([(acc_self, trans.at[2], 0, rows, 0)], half, clear=True)
    fin_send[SELF] = acc_self[theirs, :]
    finals[SELF].start()

    raw_chunk(2)
    for copy in firsts:
        copy.wait_recv()
    contract([(part_right, first, 0, rows, FIRST_FROM)], KEEP1, clear=True)
    swap_halves(RIGHT, part_right)
    finals[SELF].wait_recv()
    put(grid_at, acc_self[mine, :] + fin_recv[SELF], clear=True)
    send_back(RIGHT, part_right, back_right_send, back_right)
    raw_chunk(3)
    raw_chunk(4)
    second_chunk(0)
    raw_chunk(5)
    swap_halves(LEFT, part_left)
    second_chunk(1)
    send_back(LEFT, part_left, back_left_send, back_left)
    raw_chunk(6)

    fin_send[RIGHT] = acc_right[theirs, :]
    finals[RIGHT].start()
    second_chunk(2)
    fin_send[LEFT] = acc_left[theirs, :]
    finals[LEFT].start()
    back_right.wait_recv()
    finals[RIGHT].wait_recv()
    put(right, acc_right[mine, :] + ret_right[...].astype(F32) + fin_recv[RIGHT])
    back_left.wait_recv()
    finals[LEFT].wait_recv()
    put(left, acc_left[mine, :] + ret_left[...].astype(F32) + fin_recv[LEFT])

    for copy in [greens, *siblings, *raws, *firsts, *seconds, *halves, back_right, back_left, *finals]:
        copy.wait_send()


COPIES = 1 + 2 * P_CHUNKS + len(RAW_BOUNDS) + len(SECOND_BOUNDS) - 2 + 4 + 3


def on_device(tensor, go_blocks, gv_blocks, partners):
    _, ri, half, _ = tensor.shape
    share = ri // 2
    square = pltpu.VMEM((ri, ri), F32)
    narrow = pltpu.VMEM((share, ri), BF)
    blocks = pltpu.VMEM((2, BS, BS), BF)
    green_rows = pltpu.VMEM((BS + half, BS), BF)
    result = pl.pallas_call(
        kernel,
        out_shape=jax.ShapeDtypeStruct((2, share, ri), F32),
        in_specs=[pl.BlockSpec(memory_space=pl.ANY)] * 3 + [pl.BlockSpec(memory_space=pltpu.SMEM)],
        out_specs=pl.BlockSpec(memory_space=pltpu.VMEM),
        scratch_shapes=[
            pltpu.VMEM((2, ri, half, BS), BF),
            pltpu.VMEM((half, ri, BS), BF),
            pltpu.VMEM((half - KEEP1, ri, BS), BF),
            pltpu.VMEM((ri, 3 * half, BS), BF),
            pltpu.VMEM((3, half, ri, BS), BF),
            pltpu.VMEM((3, 2 * BS, 2 * BS), BF),
            pltpu.VMEM((256, 256), BF),
            pltpu.VMEM((3 * half, BS), BF),
            blocks, blocks, green_rows, green_rows,
            pltpu.VMEM((KEEP1, ri, BS), BF),
            pltpu.VMEM((KEEP2, ri, BS), BF),
            square, square, square, square, square,
            pltpu.VMEM((2, share, ri), F32),
            pltpu.VMEM((2, share, ri), F32),
            narrow, narrow, narrow, narrow,
            pltpu.VMEM((3, share, ri), F32),
            pltpu.VMEM((3, share, ri), F32),
            pltpu.SemaphoreType.DMA((4,)),
            pltpu.SemaphoreType.DMA((COPIES,)),
            pltpu.SemaphoreType.DMA((COPIES,)),
        ],
        compiler_params=pltpu.CompilerParams(
            collective_id=0, has_side_effects=True, vmem_limit_bytes=52 * 1024 * 1024
        ),
    )(tensor, go_blocks, gv_blocks, partners)
    return result[None]


def solution(mesh):
    placed = (
        P("grid", None, "remap", None),
        P("grid", None, None, None),
        P("grid", None, None, None),
        P("grid", None),
    )
    return jax.shard_map(
        on_device,
        mesh=mesh,
        in_specs=placed,
        out_specs=P("grid", None, "remap", None),
        check_vma=False,
    )
```

```python
import jax
import jax.numpy as jnp
from jax import lax
from jax.experimental import pallas as pl
from jax.experimental.pallas import tpu as pltpu
from jax.sharding import PartitionSpec as P

MESH = pl.DeviceIdType.MESH
BF = jnp.bfloat16
F32 = jnp.float32
BS = 128

KEEP1 = 20
KEEP2 = 22
RAW_BOUNDS = (0, 8, 16, 24, 32, 38, 42, 44)
FIRST_FROM = 64 - KEEP1
SECOND_BOUNDS = (42, 52, 60, 64)
P_BOUNDS = (0, 32, 64, 128, 256)
P_CHUNKS = len(P_BOUNDS) - 1

RIGHT, LEFT, SELF = 0, 1, 2


def nt(a, b):
    return lax.dot_general(a, b, (((1,), (1,)), ((), ())), preferred_element_type=F32)


def kernel(
    tensor, go_hbm, gv_hbm, partners_hbm, out,
    traw, rows, far, occ, trans, got2, perm, green, partners, go_ref, gv_ref, gsend, gfar, first, second,
    acc_right, acc_left, acc_self, part_right, part_left,
    half_send, half_recv, back_right_send, back_left_send, ret_right, ret_left,
    fin_send, fin_recv, load_sem, send_sem, recv_sem,
):
    half = rows.shape[0]
    ri = rows.shape[1]
    share = ri // 2
    count = lax.axis_size("grid")
    grid_at = lax.axis_index("grid")
    core = lax.axis_index("remap")
    right = lax.rem(grid_at + 1, count)
    left = lax.rem(grid_at + count - 1, count)
    other = 1 - core

    barrier = pltpu.get_barrier_semaphore()
    for target in ({"grid": left}, {"grid": right}, {"remap": other}):
        pl.semaphore_signal(barrier, inc=1, device_id=target, device_id_type=MESH)

    def loaded(at, n0, size):
        span = pl.ds(n0, size)
        return pltpu.make_async_copy(tensor.at[0, :, span], traw.at[core, :, span], load_sem.at[at])

    loads = [loaded(0, 0, 16), loaded(1, 16, half - 16)]
    loads += [
        pltpu.make_async_copy(partners_hbm, partners, load_sem.at[2]),
        pltpu.make_async_copy(go_hbm.at[0], go_ref, load_sem.at[3]),
        pltpu.make_async_copy(gv_hbm.at[0], gv_ref, load_sem.at[4]),
    ]
    for copy in loads[2:] + loads[:2]:
        copy.start()

    used = [0]

    def remote(source, target, device):
        at = used[0]
        used[0] += 1
        return pltpu.make_async_remote_copy(
            src_ref=source, dst_ref=target, send_sem=send_sem.at[at], recv_sem=recv_sem.at[at],
            device_id=device, device_id_type=MESH,
        )

    to_left, to_right, to_other = {"grid": left}, {"grid": right}, {"remap": other}
    greens = remote(gsend, gfar, to_left)
    theirs = pl.ds(pl.multiple_of(other * share, share), share)
    mine = pl.ds(pl.multiple_of(core * share, share), share)
    p_spans = [pl.ds(a, b - a) for a, b in zip(P_BOUNDS[:-1], P_BOUNDS[1:])]
    siblings = [
        remote(tensor.at[0, span], traw.at[core, span], to_other)
        for span in p_spans
    ]
    raws = [
        remote(rows.at[pl.ds(a, b - a)], far.at[pl.ds(a, b - a)], to_left)
        for a, b in zip(RAW_BOUNDS[:-1], RAW_BOUNDS[1:])
    ]
    firsts = [
        remote(trans.at[0, pl.ds(FIRST_FROM, KEEP1), span], first.at[:, span], to_right)
        for span in p_spans
    ]
    seconds = [
        remote(trans.at[1, pl.ds(a, b - a)], second.at[pl.ds(a - SECOND_BOUNDS[0], b - a)], to_right)
        for a, b in zip(SECOND_BOUNDS[:-1], SECOND_BOUNDS[1:])
    ]
    back_right = remote(back_right_send, ret_right, to_left)
    back_left = remote(back_left_send, ret_left, to_right)
    halves = [remote(half_send.at[d], half_recv.at[d], to_other) for d in (RIGHT, LEFT)]
    finals = [remote(fin_send.at[d], fin_recv.at[d], to_other) for d in (RIGHT, LEFT, SELF)]

    def picked(ref, target):
        total = jnp.zeros((BS, BS), F32)
        for slot in range(2):
            weight = (partners[0, slot] == target).astype(F32)
            total = total + ref[slot].astype(F32) * weight
        return total.astype(BF)

    out_row = lax.broadcasted_iota(jnp.int32, (256, 256), 0)
    in_row = lax.broadcasted_iota(jnp.int32, (256, 256), 1)
    perm[...] = (in_row == (out_row & 15) * 16 + (out_row >> 4)).astype(F32).astype(BF)

    n_at = lax.broadcasted_iota(jnp.int32, (half, BS), 0) + core * half
    n_of = lax.broadcasted_iota(jnp.int32, (half, BS), 1)
    choose = (n_at == n_of).astype(F32).astype(BF)
    for copy in loads[2:]:
        copy.wait()
    gsend[pl.ds(0, BS)] = picked(go_ref, left)
    gsend[pl.ds(BS, half)] = nt(choose, picked(gv_ref, left)).astype(BF)
    green[pl.ds(0, half)] = nt(choose, picked(go_ref, right)).astype(BF)
    green[pl.ds(2 * half, half)] = nt(choose, picked(go_ref, grid_at)).astype(BF)
    empty = jnp.zeros((BS, BS), BF)

    def doubled(block):
        top = jnp.concatenate([block, empty], axis=1)
        bottom = jnp.concatenate([empty, block], axis=1)
        return jnp.concatenate([top, bottom], axis=0)

    got2[0] = doubled(picked(gv_ref, right))
    got2[2] = doubled(picked(gv_ref, grid_at))

    def turn(n_blocks):
        width = 64 if len(n_blocks) == 1 else 32

        def body(i, carry):
            for n0 in n_blocks:
                for u in range(width // 32):
                    q0 = pl.multiple_of(i * width + u * 32, 32)
                    pair = [
                        traw[core, pl.ds(q0 + 16 * j, 16), pl.ds(n0, 16), :].reshape(256, BS) for j in range(2)
                    ]
                    turned = jnp.dot(
                        perm[...], jnp.concatenate(pair, axis=1), preferred_element_type=F32
                    ).astype(BF)
                    for j in range(2):
                        rows[pl.ds(n0, 16), pl.ds(q0 + 16 * j, 16), :] = (
                            turned[:, j * BS:(j + 1) * BS].reshape(16, 16, BS)
                        )
            return carry

        lax.fori_loop(0, ri // width, body, 0)

    loads[0].wait()
    turn([0])

    pl.semaphore_wait(barrier, 3)
    greens.start()
    siblings[0].start()
    raws[0].start()
    for copy in siblings[1:]:
        copy.start()
    raws[1].start()
    loads[1].wait()

    greens.wait_recv()
    green[pl.ds(half, half)] = gfar[pl.ds(BS, half)]
    got2[1] = doubled(gfar[pl.ds(0, BS)])

    def first_product(i, carry):
        p0 = pl.multiple_of(i * 8, 8)
        tiles = []
        for j in range(8):
            tiles.append(traw[0, p0 + j])
            tiles.append(traw[1, p0 + j])
        product = nt(green[...], jnp.concatenate(tiles, axis=0)).astype(BF)
        for j in range(8):
            occ[p0 + j] = product[:, j * BS:(j + 1) * BS]
        return carry

    def second_product(parts, start, size):
        width = 32 if len(parts) > 1 or size == 32 else 64

        def body(i, carry):
            for direction, n0 in parts:
                for u in range(width // 16):
                    p0 = pl.multiple_of(i * width + u * 16, 16)
                    pair = [
                        occ[pl.ds(p0, 16), pl.ds(direction * half + n0 + 16 * j, 16), :].reshape(256, BS)
                        for j in range(2)
                    ]
                    turned = jnp.dot(
                        perm[...], jnp.concatenate(pair, axis=1), preferred_element_type=F32
                    ).astype(BF)
                    product = nt(turned, got2[direction]).astype(BF)
                    for j in range(2):
                        trans[direction, pl.ds(n0 + 16 * j, 16), pl.ds(p0, 16), :] = (
                            product[:, j * BS:(j + 1) * BS].reshape(16, 16, BS)
                        )
            return carry

        lax.fori_loop(start // width, (start + size) // width, body, 0)

    for i in range(P_CHUNKS):
        siblings[i].wait_recv()
        a, b = P_BOUNDS[i], P_BOUNDS[i + 1]
        lax.fori_loop(a // 8, b // 8, first_product, 0)
        second_product([(0, 32)], a, b - a)
        firsts[i].start()
    turn([16])
    raws[2].start()
    second_product([(1, 32)], 0, ri)
    seconds[0].start()
    turn([32, 48])
    raws[3].start()
    raws[4].start()

    def wide(ref, at, many):
        return jnp.concatenate([ref[at + j] for j in range(many)], axis=1)

    def contract(jobs, size, clear=False):
        if clear:
            for acc, *_ in jobs:
                acc[...] = jnp.zeros_like(acc)
        groups, rest = divmod(size, 8)

        def add(at, many):
            for acc, x, x0, y, y0 in jobs:
                acc[...] += nt(wide(x, x0 + at, many), wide(y, y0 + at, many))

        def body(i, carry):
            add(8 * i, 8)
            return carry

        if groups > 1:
            lax.fori_loop(0, groups, body, 0)
        elif groups:
            add(0, 8)
        if rest:
            add(8 * groups, rest)

    second_product([(0, 0), (1, 0)], 0, ri)

    def swap_halves(direction, part):
        half_send[direction] = part[theirs, :]
        halves[direction].start()

    def send_back(direction, part, narrow, copy):
        halves[direction].wait_recv()
        narrow[...] = (part[mine, :] + half_recv[direction]).astype(BF)
        copy.start()

    def put(target, total, clear=False):
        for slot in range(2):
            term = total * (partners[0, slot] == target).astype(F32)
            out[slot] = term if clear else out[slot] + term

    def raw_chunk(i):
        a, b = RAW_BOUNDS[i], RAW_BOUNDS[i + 1]
        raws[i].wait_recv()
        jobs = [(acc_right, trans.at[0], a, far, a)]
        if b <= SECOND_BOUNDS[0]:
            jobs.append((part_left, far, a, trans.at[1], a))
        contract(jobs, b - a, clear=i == 0)

    def second_chunk(i):
        a, b = SECOND_BOUNDS[i], SECOND_BOUNDS[i + 1]
        seconds[i].wait_recv()
        contract([(acc_left, rows, a, second, a - SECOND_BOUNDS[0])], b - a, clear=i == 0)

    raw_chunk(0)
    raws[5].start()
    seconds[1].start()
    second_product([(2, 32), (2, 0)], 0, ri)
    raw_chunk(1)
    raws[6].start()
    seconds[2].start()
    contract([(acc_self, trans.at[2], 0, rows, 0)], half, clear=True)
    fin_send[SELF] = acc_self[theirs, :]
    finals[SELF].start()

    raw_chunk(2)
    for copy in firsts:
        copy.wait_recv()
    contract([(part_right, first, 0, rows, FIRST_FROM)], KEEP1, clear=True)
    swap_halves(RIGHT, part_right)
    finals[SELF].wait_recv()
    put(grid_at, acc_self[mine, :] + fin_recv[SELF], clear=True)
    send_back(RIGHT, part_right, back_right_send, back_right)
    raw_chunk(3)
    raw_chunk(4)
    second_chunk(0)
    raw_chunk(5)
    swap_halves(LEFT, part_left)
    second_chunk(1)
    send_back(LEFT, part_left, back_left_send, back_left)
    def last(x, x0, y, y0, many, span):
        left_side = jnp.concatenate([x[x0 + j, span, :] for j in range(many)], axis=1)
        return nt(left_side, wide(y, y0, many))

    a, b = RAW_BOUNDS[-2], RAW_BOUNDS[-1]
    right_end = (trans.at[0], a, far, a, b - a)
    raws[-1].wait_recv()
    fin_send[RIGHT] = acc_right[theirs, :] + last(*right_end, theirs)
    finals[RIGHT].start()
    a, b = SECOND_BOUNDS[-2], SECOND_BOUNDS[-1]
    left_end = (rows, a, second, a - SECOND_BOUNDS[0], b - a)
    seconds[-1].wait_recv()
    fin_send[LEFT] = acc_left[theirs, :] + last(*left_end, theirs)
    finals[LEFT].start()
    acc_right[mine, :] += last(*right_end, mine)
    acc_left[mine, :] += last(*left_end, mine)
    back_right.wait_recv()
    finals[RIGHT].wait_recv()
    put(right, acc_right[mine, :] + ret_right[...].astype(F32) + fin_recv[RIGHT])
    back_left.wait_recv()
    finals[LEFT].wait_recv()
    put(left, acc_left[mine, :] + ret_left[...].astype(F32) + fin_recv[LEFT])

    for copy in [greens, *siblings, *raws, *firsts, *seconds, *halves, back_right, back_left, *finals]:
        copy.wait_send()


COPIES = 1 + 2 * P_CHUNKS + len(RAW_BOUNDS) + len(SECOND_BOUNDS) - 2 + 4 + 3


def on_device(tensor, go_blocks, gv_blocks, partners):
    _, ri, half, _ = tensor.shape
    share = ri // 2
    square = pltpu.VMEM((ri, ri), F32)
    operands = (tensor, go_blocks, gv_blocks, partners)
    placed = [pltpu.with_memory_space_constraint(x, pltpu.HBM) for x in operands]
    narrow = pltpu.VMEM((share, ri), BF)
    blocks = pltpu.VMEM((2, BS, BS), BF)
    green_rows = pltpu.VMEM((BS + half, BS), BF)
    result = pl.pallas_call(
        kernel,
        out_shape=jax.ShapeDtypeStruct((2, share, ri), F32),
        in_specs=[pl.BlockSpec(memory_space=pl.ANY)] * 4,
        out_specs=pl.BlockSpec(memory_space=pltpu.VMEM),
        scratch_shapes=[
            pltpu.VMEM((2, ri, half, BS), BF),
            pltpu.VMEM((half, ri, BS), BF),
            pltpu.VMEM((half - KEEP1, ri, BS), BF),
            pltpu.VMEM((ri, 3 * half, BS), BF),
            pltpu.VMEM((3, half, ri, BS), BF),
            pltpu.VMEM((3, 2 * BS, 2 * BS), BF),
            pltpu.VMEM((256, 256), BF),
            pltpu.VMEM((3 * half, BS), BF),
            pltpu.SMEM((1, 2), jnp.int32),
            blocks, blocks, green_rows, green_rows,
            pltpu.VMEM((KEEP1, ri, BS), BF),
            pltpu.VMEM((KEEP2, ri, BS), BF),
            square, square, square, square, square,
            pltpu.VMEM((2, share, ri), F32),
            pltpu.VMEM((2, share, ri), F32),
            narrow, narrow, narrow, narrow,
            pltpu.VMEM((3, share, ri), F32),
            pltpu.VMEM((3, share, ri), F32),
            pltpu.SemaphoreType.DMA((5,)),
            pltpu.SemaphoreType.DMA((COPIES,)),
            pltpu.SemaphoreType.DMA((COPIES,)),
        ],
        compiler_params=pltpu.CompilerParams(
            collective_id=0, has_side_effects=True, vmem_limit_bytes=52 * 1024 * 1024
        ),
    )(*placed)
    return result[None]


def solution(mesh):
    placed = (
        P("grid", None, "remap", None),
        P("grid", None, None, None),
        P("grid", None, None, None),
        P("grid", None),
    )
    return jax.shard_map(
        on_device,
        mesh=mesh,
        in_specs=placed,
        out_specs=P("grid", None, "remap", None),
        check_vma=False,
    )
```

```python
import jax
import jax.numpy as jnp
from jax import lax
from jax.experimental import pallas as pl
from jax.experimental.pallas import tpu as pltpu
from jax.sharding import PartitionSpec as P

MESH = pl.DeviceIdType.MESH
BF = jnp.bfloat16
F32 = jnp.float32
BS = 128

KEEP1 = 20
KEEP2 = 23
RAW_BOUNDS = (0, 8, 16, 24, 32, 38, 41, 44)
RAW_NEXT = {0: 3, 1: 4, 3: 5, 4: 6}
FIRST_FROM = 64 - KEEP1
SECOND_BOUNDS = (41, 52, 60, 64)
P_BOUNDS = (0, 32, 64, 128, 256)
P_CHUNKS = len(P_BOUNDS) - 1

RIGHT, LEFT, SELF = 0, 1, 2


def nt(a, b):
    return lax.dot_general(a, b, (((1,), (1,)), ((), ())), preferred_element_type=F32)


def kernel(
    tensor, go_hbm, gv_hbm, partners_hbm, out,
    traw, rows, far, occ, trans, got2, perm, green, partners, go_ref, gv_ref, gsend, gfar, first, second,
    acc_right, acc_left, acc_self, part_right, part_left,
    half_send, half_recv, back_right_send, back_left_send, ret_right, ret_left,
    fin_send, fin_recv, load_sem, send_sem, recv_sem,
):
    half = rows.shape[0]
    ri = rows.shape[1]
    share = ri // 2
    count = lax.axis_size("grid")
    grid_at = lax.axis_index("grid")
    core = lax.axis_index("remap")
    right = lax.rem(grid_at + 1, count)
    left = lax.rem(grid_at + count - 1, count)
    other = 1 - core

    barrier = pltpu.get_barrier_semaphore()
    for target in ({"grid": left}, {"grid": right}, {"remap": other}):
        pl.semaphore_signal(barrier, inc=1, device_id=target, device_id_type=MESH)

    def loaded(at, n0, size):
        span = pl.ds(n0, size)
        return pltpu.make_async_copy(tensor.at[0, :, span], traw.at[core, :, span], load_sem.at[at])

    loads = [loaded(0, 0, 16), loaded(1, 16, half - 16)]
    loads += [
        pltpu.make_async_copy(partners_hbm, partners, load_sem.at[2]),
        pltpu.make_async_copy(go_hbm.at[0], go_ref, load_sem.at[3]),
        pltpu.make_async_copy(gv_hbm.at[0], gv_ref, load_sem.at[4]),
    ]
    for copy in loads[2:] + loads[:2]:
        copy.start()

    used = [0]

    def remote(source, target, device):
        at = used[0]
        used[0] += 1
        return pltpu.make_async_remote_copy(
            src_ref=source, dst_ref=target, send_sem=send_sem.at[at], recv_sem=recv_sem.at[at],
            device_id=device, device_id_type=MESH,
        )

    to_left, to_right, to_other = {"grid": left}, {"grid": right}, {"remap": other}
    greens = remote(gsend, gfar, to_left)
    theirs = pl.ds(pl.multiple_of(other * share, share), share)
    mine = pl.ds(pl.multiple_of(core * share, share), share)
    p_spans = [pl.ds(a, b - a) for a, b in zip(P_BOUNDS[:-1], P_BOUNDS[1:])]
    siblings = [
        remote(tensor.at[0, span], traw.at[core, span], to_other)
        for span in p_spans
    ]
    raws = [
        remote(rows.at[pl.ds(a, b - a)], far.at[pl.ds(a, b - a)], to_left)
        for a, b in zip(RAW_BOUNDS[:-1], RAW_BOUNDS[1:])
    ]
    firsts = [
        remote(trans.at[0, pl.ds(FIRST_FROM, KEEP1), span], first.at[:, span], to_right)
        for span in p_spans
    ]
    seconds = [
        remote(trans.at[1, pl.ds(a, b - a)], second.at[pl.ds(a - SECOND_BOUNDS[0], b - a)], to_right)
        for a, b in zip(SECOND_BOUNDS[:-1], SECOND_BOUNDS[1:])
    ]
    back_right = remote(back_right_send, ret_right, to_left)
    back_left = remote(back_left_send, ret_left, to_right)
    halves = [remote(half_send.at[d], half_recv.at[d], to_other) for d in (RIGHT, LEFT)]
    finals = [remote(fin_send.at[d], fin_recv.at[d], to_other) for d in (RIGHT, LEFT, SELF)]

    def picked(ref, target):
        total = jnp.zeros((BS, BS), F32)
        for slot in range(2):
            weight = (partners[0, slot] == target).astype(F32)
            total = total + ref[slot].astype(F32) * weight
        return total.astype(BF)

    out_row = lax.broadcasted_iota(jnp.int32, (256, 256), 0)
    in_row = lax.broadcasted_iota(jnp.int32, (256, 256), 1)
    perm[...] = (in_row == (out_row & 15) * 16 + (out_row >> 4)).astype(F32).astype(BF)

    n_at = lax.broadcasted_iota(jnp.int32, (half, BS), 0) + core * half
    n_of = lax.broadcasted_iota(jnp.int32, (half, BS), 1)
    choose = (n_at == n_of).astype(F32).astype(BF)
    for copy in loads[2:]:
        copy.wait()
    gsend[pl.ds(0, BS)] = picked(go_ref, left)
    gsend[pl.ds(BS, half)] = nt(choose, picked(gv_ref, left)).astype(BF)
    green[pl.ds(0, half)] = nt(choose, picked(go_ref, right)).astype(BF)
    green[pl.ds(2 * half, half)] = nt(choose, picked(go_ref, grid_at)).astype(BF)
    empty = jnp.zeros((BS, BS), BF)

    def doubled(block):
        top = jnp.concatenate([block, empty], axis=1)
        bottom = jnp.concatenate([empty, block], axis=1)
        return jnp.concatenate([top, bottom], axis=0)

    got2[0] = doubled(picked(gv_ref, right))
    got2[2] = doubled(picked(gv_ref, grid_at))

    def turn(n_blocks):
        width = 64 if len(n_blocks) == 1 else 32

        def body(i, carry):
            for n0 in n_blocks:
                for u in range(width // 32):
                    q0 = pl.multiple_of(i * width + u * 32, 32)
                    pair = [
                        traw[core, pl.ds(q0 + 16 * j, 16), pl.ds(n0, 16), :].reshape(256, BS) for j in range(2)
                    ]
                    turned = jnp.dot(
                        perm[...], jnp.concatenate(pair, axis=1), preferred_element_type=F32
                    ).astype(BF)
                    for j in range(2):
                        rows[pl.ds(n0, 16), pl.ds(q0 + 16 * j, 16), :] = (
                            turned[:, j * BS:(j + 1) * BS].reshape(16, 16, BS)
                        )
            return carry

        lax.fori_loop(0, ri // width, body, 0)

    loads[0].wait()
    turn([0])

    pl.semaphore_wait(barrier, 3)
    greens.start()
    siblings[0].start()
    raws[0].start()
    for copy in siblings[1:]:
        copy.start()
    raws[1].start()
    loads[1].wait()

    greens.wait_recv()
    green[pl.ds(half, half)] = gfar[pl.ds(BS, half)]
    got2[1] = doubled(gfar[pl.ds(0, BS)])

    def first_product(i, carry):
        p0 = pl.multiple_of(i * 8, 8)
        tiles = []
        for j in range(8):
            tiles.append(traw[0, p0 + j])
            tiles.append(traw[1, p0 + j])
        product = nt(green[...], jnp.concatenate(tiles, axis=0)).astype(BF)
        for j in range(8):
            occ[p0 + j] = product[:, j * BS:(j + 1) * BS]
        return carry

    def second_product(parts, start, size):
        width = 32 if len(parts) > 1 or size == 32 else 64

        def body(i, carry):
            for direction, n0 in parts:
                for u in range(width // 16):
                    p0 = pl.multiple_of(i * width + u * 16, 16)
                    pair = [
                        occ[pl.ds(p0, 16), pl.ds(direction * half + n0 + 16 * j, 16), :].reshape(256, BS)
                        for j in range(2)
                    ]
                    turned = jnp.dot(
                        perm[...], jnp.concatenate(pair, axis=1), preferred_element_type=F32
                    ).astype(BF)
                    product = nt(turned, got2[direction]).astype(BF)
                    for j in range(2):
                        trans[direction, pl.ds(n0 + 16 * j, 16), pl.ds(p0, 16), :] = (
                            product[:, j * BS:(j + 1) * BS].reshape(16, 16, BS)
                        )
            return carry

        lax.fori_loop(start // width, (start + size) // width, body, 0)

    for i in range(P_CHUNKS):
        siblings[i].wait_recv()
        a, b = P_BOUNDS[i], P_BOUNDS[i + 1]
        lax.fori_loop(a // 8, b // 8, first_product, 0)
        second_product([(0, 32)], a, b - a)
        firsts[i].start()
    turn([16])
    raws[2].start()
    second_product([(1, 32)], 0, ri)
    seconds[0].start()
    turn([32, 48])
    raws[0].wait_recv()
    raws[RAW_NEXT[0]].start()

    def wide(ref, at, many):
        return jnp.concatenate([ref[at + j] for j in range(many)], axis=1)

    def contract(jobs, size, clear=False):
        if clear:
            for acc, *_ in jobs:
                acc[...] = jnp.zeros_like(acc)
        groups, rest = divmod(size, 8)

        def add(at, many):
            for acc, x, x0, y, y0 in jobs:
                acc[...] += nt(wide(x, x0 + at, many), wide(y, y0 + at, many))

        def body(i, carry):
            add(8 * i, 8)
            return carry

        if groups > 1:
            lax.fori_loop(0, groups, body, 0)
        elif groups:
            add(0, 8)
        if rest:
            add(8 * groups, rest)

    second_product([(0, 0), (1, 0)], 0, ri)

    def swap_halves(direction, part):
        half_send[direction] = part[theirs, :]
        halves[direction].start()

    def send_back(direction, part, narrow, copy):
        halves[direction].wait_recv()
        narrow[...] = (part[mine, :] + half_recv[direction]).astype(BF)
        copy.start()

    def put(target, total, clear=False):
        for slot in range(2):
            term = total * (partners[0, slot] == target).astype(F32)
            out[slot] = term if clear else out[slot] + term

    def raw_chunk(i):
        a, b = RAW_BOUNDS[i], RAW_BOUNDS[i + 1]
        if i > 0:
            raws[i].wait_recv()
            if i in RAW_NEXT:
                raws[RAW_NEXT[i]].start()
        jobs = [(acc_right, trans.at[0], a, far, a)]
        if b <= SECOND_BOUNDS[0]:
            jobs.append((part_left, far, a, trans.at[1], a))
        contract(jobs, b - a, clear=i == 0)

    def second_chunk(i):
        a, b = SECOND_BOUNDS[i], SECOND_BOUNDS[i + 1]
        seconds[i].wait_recv()
        contract([(acc_left, rows, a, second, a - SECOND_BOUNDS[0])], b - a, clear=i == 0)

    raw_chunk(0)
    raw_chunk(1)
    seconds[1].start()
    second_product([(2, 32), (2, 0)], 0, ri)
    raw_chunk(2)
    seconds[2].start()
    contract([(acc_self, trans.at[2], 0, rows, 0)], half, clear=True)
    fin_send[SELF] = acc_self[theirs, :]
    finals[SELF].start()

    for copy in firsts:
        copy.wait_recv()
    contract([(part_right, first, 0, rows, FIRST_FROM)], KEEP1, clear=True)
    swap_halves(RIGHT, part_right)
    finals[SELF].wait_recv()
    put(grid_at, acc_self[mine, :] + fin_recv[SELF], clear=True)
    send_back(RIGHT, part_right, back_right_send, back_right)
    raw_chunk(3)
    raw_chunk(4)
    second_chunk(0)
    raw_chunk(5)
    swap_halves(LEFT, part_left)
    second_chunk(1)
    send_back(LEFT, part_left, back_left_send, back_left)
    def last(x, x0, y, y0, many, span):
        left_side = jnp.concatenate([x[x0 + j, span, :] for j in range(many)], axis=1)
        return nt(left_side, wide(y, y0, many))

    a, b = RAW_BOUNDS[-2], RAW_BOUNDS[-1]
    right_end = (trans.at[0], a, far, a, b - a)
    raws[-1].wait_recv()
    fin_send[RIGHT] = acc_right[theirs, :] + last(*right_end, theirs)
    finals[RIGHT].start()
    a, b = SECOND_BOUNDS[-2], SECOND_BOUNDS[-1]
    left_end = (rows, a, second, a - SECOND_BOUNDS[0], b - a)
    seconds[-1].wait_recv()
    fin_send[LEFT] = acc_left[theirs, :] + last(*left_end, theirs)
    finals[LEFT].start()
    acc_right[mine, :] += last(*right_end, mine)
    acc_left[mine, :] += last(*left_end, mine)
    back_right.wait_recv()
    finals[RIGHT].wait_recv()
    put(right, acc_right[mine, :] + ret_right[...].astype(F32) + fin_recv[RIGHT])
    back_left.wait_recv()
    finals[LEFT].wait_recv()
    put(left, acc_left[mine, :] + ret_left[...].astype(F32) + fin_recv[LEFT])

    for copy in [greens, *siblings, *raws, *firsts, *seconds, *halves, back_right, back_left, *finals]:
        copy.wait_send()


COPIES = 1 + 2 * P_CHUNKS + len(RAW_BOUNDS) + len(SECOND_BOUNDS) - 2 + 4 + 3


def on_device(tensor, go_blocks, gv_blocks, partners):
    _, ri, half, _ = tensor.shape
    share = ri // 2
    square = pltpu.VMEM((ri, ri), F32)
    operands = (tensor, go_blocks, gv_blocks, partners)
    placed = [pltpu.with_memory_space_constraint(x, pltpu.HBM) for x in operands]
    narrow = pltpu.VMEM((share, ri), BF)
    blocks = pltpu.VMEM((2, BS, BS), BF)
    green_rows = pltpu.VMEM((BS + half, BS), BF)
    result = pl.pallas_call(
        kernel,
        out_shape=jax.ShapeDtypeStruct((2, share, ri), F32),
        in_specs=[pl.BlockSpec(memory_space=pl.ANY)] * 4,
        out_specs=pl.BlockSpec(memory_space=pltpu.VMEM),
        scratch_shapes=[
            pltpu.VMEM((2, ri, half, BS), BF),
            pltpu.VMEM((half, ri, BS), BF),
            pltpu.VMEM((half - KEEP1, ri, BS), BF),
            pltpu.VMEM((ri, 3 * half, BS), BF),
            pltpu.VMEM((3, half, ri, BS), BF),
            pltpu.VMEM((3, 2 * BS, 2 * BS), BF),
            pltpu.VMEM((256, 256), BF),
            pltpu.VMEM((3 * half, BS), BF),
            pltpu.SMEM((1, 2), jnp.int32),
            blocks, blocks, green_rows, green_rows,
            pltpu.VMEM((KEEP1, ri, BS), BF),
            pltpu.VMEM((KEEP2, ri, BS), BF),
            square, square, square, square, square,
            pltpu.VMEM((2, share, ri), F32),
            pltpu.VMEM((2, share, ri), F32),
            narrow, narrow, narrow, narrow,
            pltpu.VMEM((3, share, ri), F32),
            pltpu.VMEM((3, share, ri), F32),
            pltpu.SemaphoreType.DMA((5,)),
            pltpu.SemaphoreType.DMA((COPIES,)),
            pltpu.SemaphoreType.DMA((COPIES,)),
        ],
        compiler_params=pltpu.CompilerParams(
            collective_id=0, has_side_effects=True, vmem_limit_bytes=52 * 1024 * 1024
        ),
    )(*placed)
    return result[None]


def solution(mesh):
    placed = (
        P("grid", None, "remap", None),
        P("grid", None, None, None),
        P("grid", None, None, None),
        P("grid", None),
    )
    return jax.shard_map(
        on_device,
        mesh=mesh,
        in_specs=placed,
        out_specs=P("grid", None, "remap", None),
        check_vma=False,
    )
```

```python
import jax
import jax.numpy as jnp
from jax import lax
from jax.experimental import pallas as pl
from jax.experimental.pallas import tpu as pltpu
from jax.sharding import PartitionSpec as P

MESH = pl.DeviceIdType.MESH
BF = jnp.bfloat16
F32 = jnp.float32
BS = 128

KEEP1 = 20
KEEP2 = 22
RAW_BOUNDS = (0, 8, 16, 24, 32, 38, 42, 44)
FIRST_FROM = 64 - KEEP1
SECOND_BOUNDS = (42, 52, 60, 64)
P_BOUNDS = (0, 16, 32, 64, 128, 256)
P_CHUNKS = len(P_BOUNDS) - 1
EARLY_CHUNKS = 2

RIGHT, LEFT, SELF = 0, 1, 2


def nt(a, b):
    return lax.dot_general(a, b, (((1,), (1,)), ((), ())), preferred_element_type=F32)


def kernel(
    tensor, go_hbm, gv_hbm, partners_hbm, out,
    traw, rows, far, occ, trans, got2, perm, green, partners, go_ref, gv_ref, gsend, gfar, first, second,
    acc_right, acc_left, acc_self, part_right, part_left,
    half_send, half_recv, back_right_send, back_left_send, ret_right, ret_left,
    fin_send, fin_recv, load_sem, send_sem, recv_sem,
):
    half = rows.shape[0]
    ri = rows.shape[1]
    share = ri // 2
    count = lax.axis_size("grid")
    grid_at = lax.axis_index("grid")
    core = lax.axis_index("remap")
    right = lax.rem(grid_at + 1, count)
    left = lax.rem(grid_at + count - 1, count)
    other = 1 - core

    barrier = pltpu.get_barrier_semaphore()
    for target in ({"grid": left}, {"grid": right}, {"remap": other}):
        pl.semaphore_signal(barrier, inc=1, device_id=target, device_id_type=MESH)

    def loaded(at, n0, size):
        span = pl.ds(n0, size)
        return pltpu.make_async_copy(tensor.at[0, :, span], traw.at[core, :, span], load_sem.at[at])

    loads = [loaded(0, 0, 16), loaded(1, 16, half - 16)]
    loads += [
        pltpu.make_async_copy(partners_hbm, partners, load_sem.at[2]),
        pltpu.make_async_copy(go_hbm.at[0], go_ref, load_sem.at[3]),
        pltpu.make_async_copy(gv_hbm.at[0], gv_ref, load_sem.at[4]),
    ]
    for copy in loads[2:] + loads[:2]:
        copy.start()

    used = [0]

    def remote(source, target, device):
        at = used[0]
        used[0] += 1
        return pltpu.make_async_remote_copy(
            src_ref=source, dst_ref=target, send_sem=send_sem.at[at], recv_sem=recv_sem.at[at],
            device_id=device, device_id_type=MESH,
        )

    to_left, to_right, to_other = {"grid": left}, {"grid": right}, {"remap": other}
    greens = remote(gsend, gfar, to_left)
    theirs = pl.ds(pl.multiple_of(other * share, share), share)
    mine = pl.ds(pl.multiple_of(core * share, share), share)
    p_spans = [pl.ds(a, b - a) for a, b in zip(P_BOUNDS[:-1], P_BOUNDS[1:])]
    siblings = [
        remote(tensor.at[0, span], traw.at[core, span], to_other)
        for span in p_spans
    ]
    raws = [
        remote(rows.at[pl.ds(a, b - a)], far.at[pl.ds(a, b - a)], to_left)
        for a, b in zip(RAW_BOUNDS[:-1], RAW_BOUNDS[1:])
    ]
    firsts = [
        remote(trans.at[0, pl.ds(FIRST_FROM, KEEP1), span], first.at[:, span], to_right)
        for span in p_spans
    ]
    seconds = [
        remote(trans.at[1, pl.ds(a, b - a)], second.at[pl.ds(a - SECOND_BOUNDS[0], b - a)], to_right)
        for a, b in zip(SECOND_BOUNDS[:-1], SECOND_BOUNDS[1:])
    ]
    back_right = remote(back_right_send, ret_right, to_left)
    back_left = remote(back_left_send, ret_left, to_right)
    halves = [remote(half_send.at[d], half_recv.at[d], to_other) for d in (RIGHT, LEFT)]
    finals = [remote(fin_send.at[d], fin_recv.at[d], to_other) for d in (RIGHT, LEFT, SELF)]

    def picked(ref, target):
        total = jnp.zeros((BS, BS), F32)
        for slot in range(2):
            weight = (partners[0, slot] == target).astype(F32)
            total = total + ref[slot].astype(F32) * weight
        return total.astype(BF)

    out_row = lax.broadcasted_iota(jnp.int32, (256, 256), 0)
    in_row = lax.broadcasted_iota(jnp.int32, (256, 256), 1)
    perm[...] = (in_row == (out_row & 15) * 16 + (out_row >> 4)).astype(F32).astype(BF)

    n_at = lax.broadcasted_iota(jnp.int32, (half, BS), 0) + core * half
    n_of = lax.broadcasted_iota(jnp.int32, (half, BS), 1)
    choose = (n_at == n_of).astype(F32).astype(BF)
    for copy in loads[2:]:
        copy.wait()
    gsend[pl.ds(0, BS)] = picked(go_ref, left)
    gsend[pl.ds(BS, half)] = nt(choose, picked(gv_ref, left)).astype(BF)
    def turn(n_blocks):
        width = 64 if len(n_blocks) == 1 else 32

        def body(i, carry):
            for n0 in n_blocks:
                for u in range(width // 32):
                    q0 = pl.multiple_of(i * width + u * 32, 32)
                    pair = [
                        traw[core, pl.ds(q0 + 16 * j, 16), pl.ds(n0, 16), :].reshape(256, BS) for j in range(2)
                    ]
                    turned = jnp.dot(
                        perm[...], jnp.concatenate(pair, axis=1), preferred_element_type=F32
                    ).astype(BF)
                    for j in range(2):
                        rows[pl.ds(n0, 16), pl.ds(q0 + 16 * j, 16), :] = (
                            turned[:, j * BS:(j + 1) * BS].reshape(16, 16, BS)
                        )
            return carry

        lax.fori_loop(0, ri // width, body, 0)

    loads[0].wait()
    turn([0])

    pl.semaphore_wait(barrier, 3)
    greens.start()
    siblings[0].start()
    raws[0].start()
    for copy in siblings[1:]:
        copy.start()
    raws[1].start()

    green[pl.ds(0, half)] = nt(choose, picked(go_ref, right)).astype(BF)
    green[pl.ds(2 * half, half)] = nt(choose, picked(go_ref, grid_at)).astype(BF)
    empty = jnp.zeros((BS, BS), BF)

    def doubled(block):
        top = jnp.concatenate([block, empty], axis=1)
        bottom = jnp.concatenate([empty, block], axis=1)
        return jnp.concatenate([top, bottom], axis=0)

    got2[0] = doubled(picked(gv_ref, right))
    got2[2] = doubled(picked(gv_ref, grid_at))
    loads[1].wait()

    def first_product(start, stop, row, many):
        def body(i, carry):
            p0 = pl.multiple_of(i * 8, 8)
            tiles = []
            for j in range(8):
                tiles.append(traw[0, p0 + j])
                tiles.append(traw[1, p0 + j])
            product = nt(green[pl.ds(row, many)], jnp.concatenate(tiles, axis=0)).astype(BF)
            for j in range(8):
                occ[p0 + j, pl.ds(row, many)] = product[:, j * BS:(j + 1) * BS]
            return carry

        lax.fori_loop(start // 8, stop // 8, body, 0)

    def second_product(parts, start, size):
        width = 32 if len(parts) > 1 else min(64, size)

        def body(i, carry):
            for direction, n0 in parts:
                for u in range(width // 16):
                    p0 = pl.multiple_of(i * width + u * 16, 16)
                    pair = [
                        occ[pl.ds(p0, 16), pl.ds(direction * half + n0 + 16 * j, 16), :].reshape(256, BS)
                        for j in range(2)
                    ]
                    turned = jnp.dot(
                        perm[...], jnp.concatenate(pair, axis=1), preferred_element_type=F32
                    ).astype(BF)
                    product = nt(turned, got2[direction]).astype(BF)
                    for j in range(2):
                        trans[direction, pl.ds(n0 + 16 * j, 16), pl.ds(p0, 16), :] = (
                            product[:, j * BS:(j + 1) * BS].reshape(16, 16, BS)
                        )
            return carry

        lax.fori_loop(start // width, (start + size) // width, body, 0)

    for i in range(P_CHUNKS):
        siblings[i].wait_recv()
        a, b = P_BOUNDS[i], P_BOUNDS[i + 1]
        if i == EARLY_CHUNKS:
            greens.wait_recv()
            green[pl.ds(half, half)] = gfar[pl.ds(BS, half)]
            got2[1] = doubled(gfar[pl.ds(0, BS)])
            first_product(0, a, half, 2 * half)
        if i < EARLY_CHUNKS:
            first_product(a, b, 0, half)
        else:
            first_product(a, b, 0, 3 * half)
        second_product([(0, 32)], a, b - a)
        firsts[i].start()
    turn([16])
    raws[2].start()
    second_product([(1, 32)], 0, ri)
    seconds[0].start()
    turn([32, 48])
    raws[3].start()
    raws[4].start()

    def wide(ref, at, many):
        return jnp.concatenate([ref[at + j] for j in range(many)], axis=1)

    def contract(jobs, size, clear=False):
        if clear:
            for acc, *_ in jobs:
                acc[...] = jnp.zeros_like(acc)
        groups, rest = divmod(size, 8)

        def add(at, many):
            for acc, x, x0, y, y0 in jobs:
                acc[...] += nt(wide(x, x0 + at, many), wide(y, y0 + at, many))

        def body(i, carry):
            add(8 * i, 8)
            return carry

        if groups > 1:
            lax.fori_loop(0, groups, body, 0)
        elif groups:
            add(0, 8)
        if rest:
            add(8 * groups, rest)

    second_product([(0, 0), (1, 0)], 0, ri)

    def swap_halves(direction, part):
        half_send[direction] = part[theirs, :]
        halves[direction].start()

    def send_back(direction, part, narrow, copy):
        halves[direction].wait_recv()
        narrow[...] = (part[mine, :] + half_recv[direction]).astype(BF)
        copy.start()

    def put(target, total, clear=False):
        for slot in range(2):
            term = total * (partners[0, slot] == target).astype(F32)
            out[slot] = term if clear else out[slot] + term

    def raw_chunk(i):
        a, b = RAW_BOUNDS[i], RAW_BOUNDS[i + 1]
        raws[i].wait_recv()
        jobs = [(acc_right, trans.at[0], a, far, a)]
        if b <= SECOND_BOUNDS[0]:
            jobs.append((part_left, far, a, trans.at[1], a))
        contract(jobs, b - a, clear=i == 0)

    def second_chunk(i):
        a, b = SECOND_BOUNDS[i], SECOND_BOUNDS[i + 1]
        seconds[i].wait_recv()
        contract([(acc_left, rows, a, second, a - SECOND_BOUNDS[0])], b - a, clear=i == 0)

    raw_chunk(0)
    raws[5].start()
    seconds[1].start()
    second_product([(2, 32), (2, 0)], 0, ri)
    raw_chunk(1)
    raws[6].start()
    seconds[2].start()
    contract([(acc_self, trans.at[2], 0, rows, 0)], half, clear=True)
    fin_send[SELF] = acc_self[theirs, :]
    finals[SELF].start()

    raw_chunk(2)
    for copy in firsts:
        copy.wait_recv()
    contract([(part_right, first, 0, rows, FIRST_FROM)], KEEP1, clear=True)
    swap_halves(RIGHT, part_right)
    finals[SELF].wait_recv()
    put(grid_at, acc_self[mine, :] + fin_recv[SELF], clear=True)
    send_back(RIGHT, part_right, back_right_send, back_right)
    raw_chunk(3)
    raw_chunk(4)
    second_chunk(0)
    raw_chunk(5)
    swap_halves(LEFT, part_left)
    second_chunk(1)
    send_back(LEFT, part_left, back_left_send, back_left)
    def last(x, x0, y, y0, many, span):
        left_side = jnp.concatenate([x[x0 + j, span, :] for j in range(many)], axis=1)
        return nt(left_side, wide(y, y0, many))

    a, b = RAW_BOUNDS[-2], RAW_BOUNDS[-1]
    right_end = (trans.at[0], a, far, a, b - a)
    raws[-1].wait_recv()
    fin_send[RIGHT] = acc_right[theirs, :] + last(*right_end, theirs)
    finals[RIGHT].start()
    a, b = SECOND_BOUNDS[-2], SECOND_BOUNDS[-1]
    left_end = (rows, a, second, a - SECOND_BOUNDS[0], b - a)
    seconds[-1].wait_recv()
    fin_send[LEFT] = acc_left[theirs, :] + last(*left_end, theirs)
    finals[LEFT].start()
    acc_right[mine, :] += last(*right_end, mine)
    acc_left[mine, :] += last(*left_end, mine)
    back_right.wait_recv()
    finals[RIGHT].wait_recv()
    put(right, acc_right[mine, :] + ret_right[...].astype(F32) + fin_recv[RIGHT])
    back_left.wait_recv()
    finals[LEFT].wait_recv()
    put(left, acc_left[mine, :] + ret_left[...].astype(F32) + fin_recv[LEFT])

    for copy in [greens, *siblings, *raws, *firsts, *seconds, *halves, back_right, back_left, *finals]:
        copy.wait_send()


COPIES = 1 + 2 * P_CHUNKS + len(RAW_BOUNDS) + len(SECOND_BOUNDS) - 2 + 4 + 3


def on_device(tensor, go_blocks, gv_blocks, partners):
    _, ri, half, _ = tensor.shape
    share = ri // 2
    square = pltpu.VMEM((ri, ri), F32)
    operands = (tensor, go_blocks, gv_blocks, partners)
    placed = [pltpu.with_memory_space_constraint(x, pltpu.HBM) for x in operands]
    narrow = pltpu.VMEM((share, ri), BF)
    blocks = pltpu.VMEM((2, BS, BS), BF)
    green_rows = pltpu.VMEM((BS + half, BS), BF)
    result = pl.pallas_call(
        kernel,
        out_shape=jax.ShapeDtypeStruct((2, share, ri), F32),
        in_specs=[pl.BlockSpec(memory_space=pl.ANY)] * 4,
        out_specs=pl.BlockSpec(memory_space=pltpu.VMEM),
        scratch_shapes=[
            pltpu.VMEM((2, ri, half, BS), BF),
            pltpu.VMEM((half, ri, BS), BF),
            pltpu.VMEM((half - KEEP1, ri, BS), BF),
            pltpu.VMEM((ri, 3 * half, BS), BF),
            pltpu.VMEM((3, half, ri, BS), BF),
            pltpu.VMEM((3, 2 * BS, 2 * BS), BF),
            pltpu.VMEM((256, 256), BF),
            pltpu.VMEM((3 * half, BS), BF),
            pltpu.SMEM((1, 2), jnp.int32),
            blocks, blocks, green_rows, green_rows,
            pltpu.VMEM((KEEP1, ri, BS), BF),
            pltpu.VMEM((KEEP2, ri, BS), BF),
            square, square, square, square, square,
            pltpu.VMEM((2, share, ri), F32),
            pltpu.VMEM((2, share, ri), F32),
            narrow, narrow, narrow, narrow,
            pltpu.VMEM((3, share, ri), F32),
            pltpu.VMEM((3, share, ri), F32),
            pltpu.SemaphoreType.DMA((5,)),
            pltpu.SemaphoreType.DMA((COPIES,)),
            pltpu.SemaphoreType.DMA((COPIES,)),
        ],
        compiler_params=pltpu.CompilerParams(
            collective_id=0, has_side_effects=True, vmem_limit_bytes=52 * 1024 * 1024
        ),
    )(*placed)
    return result[None]


def solution(mesh):
    placed = (
        P("grid", None, "remap", None),
        P("grid", None, None, None),
        P("grid", None, None, None),
        P("grid", None),
    )
    return jax.shard_map(
        on_device,
        mesh=mesh,
        in_specs=placed,
        out_specs=P("grid", None, "remap", None),
        check_vma=False,
    )
```

```python
import jax
import jax.numpy as jnp
from jax import lax
from jax.experimental import pallas as pl
from jax.experimental.pallas import tpu as pltpu
from jax.sharding import PartitionSpec as P

MESH = pl.DeviceIdType.MESH
BF = jnp.bfloat16
F32 = jnp.float32
BS = 128

KEEP1 = 21
KEEP2 = 22
RAW_BOUNDS = (0, 8, 16, 24, 32, 38, 42, 43)
FIRST_FROM = 64 - KEEP1
SECOND_BOUNDS = (42, 52, 60, 64)
P_BOUNDS = (0, 16, 32, 64, 128, 256)
P_CHUNKS = len(P_BOUNDS) - 1
EARLY_CHUNKS = 2

RIGHT, LEFT, SELF = 0, 1, 2


def nt(a, b):
    return lax.dot_general(a, b, (((1,), (1,)), ((), ())), preferred_element_type=F32)


def kernel(
    tensor, go_hbm, gv_hbm, partners_hbm, out,
    traw, rows, far, occ, trans, got2, perm, green, partners, go_ref, gv_ref, gsend, gfar, first, second,
    acc_right, acc_left, acc_self, part_right, part_left,
    half_send, half_recv, back_right_send, back_left_send, ret_right, ret_left,
    fin_send, fin_recv, load_sem, send_sem, recv_sem,
):
    half = rows.shape[0]
    ri = rows.shape[1]
    share = ri // 2
    count = lax.axis_size("grid")
    grid_at = lax.axis_index("grid")
    core = lax.axis_index("remap")
    right = lax.rem(grid_at + 1, count)
    left = lax.rem(grid_at + count - 1, count)
    other = 1 - core

    barrier = pltpu.get_barrier_semaphore()
    for target in ({"grid": left}, {"grid": right}, {"remap": other}):
        pl.semaphore_signal(barrier, inc=1, device_id=target, device_id_type=MESH)

    def loaded(at, n0, size):
        span = pl.ds(n0, size)
        return pltpu.make_async_copy(tensor.at[0, :, span], traw.at[core, :, span], load_sem.at[at])

    loads = [loaded(0, 0, 16), loaded(1, 16, half - 16)]
    loads += [
        pltpu.make_async_copy(partners_hbm, partners, load_sem.at[2]),
        pltpu.make_async_copy(go_hbm.at[0], go_ref, load_sem.at[3]),
        pltpu.make_async_copy(gv_hbm.at[0], gv_ref, load_sem.at[4]),
    ]
    for copy in loads[2:] + loads[:2]:
        copy.start()

    used = [0]

    def remote(source, target, device):
        at = used[0]
        used[0] += 1
        return pltpu.make_async_remote_copy(
            src_ref=source, dst_ref=target, send_sem=send_sem.at[at], recv_sem=recv_sem.at[at],
            device_id=device, device_id_type=MESH,
        )

    to_left, to_right, to_other = {"grid": left}, {"grid": right}, {"remap": other}
    greens = remote(gsend, gfar, to_left)
    theirs = pl.ds(pl.multiple_of(other * share, share), share)
    mine = pl.ds(pl.multiple_of(core * share, share), share)
    p_spans = [pl.ds(a, b - a) for a, b in zip(P_BOUNDS[:-1], P_BOUNDS[1:])]
    siblings = [
        remote(tensor.at[0, span], traw.at[core, span], to_other)
        for span in p_spans
    ]
    raws = [
        remote(rows.at[pl.ds(a, b - a)], far.at[pl.ds(a, b - a)], to_left)
        for a, b in zip(RAW_BOUNDS[:-1], RAW_BOUNDS[1:])
    ]
    firsts = [
        remote(trans.at[0, pl.ds(FIRST_FROM, KEEP1), span], first.at[:, span], to_right)
        for span in p_spans
    ]
    seconds = [
        remote(trans.at[1, pl.ds(a, b - a)], second.at[pl.ds(a - SECOND_BOUNDS[0], b - a)], to_right)
        for a, b in zip(SECOND_BOUNDS[:-1], SECOND_BOUNDS[1:])
    ]
    back_right = remote(back_right_send, ret_right, to_left)
    back_left = remote(back_left_send, ret_left, to_right)
    halves = [remote(half_send.at[d], half_recv.at[d], to_other) for d in (RIGHT, LEFT)]
    finals = [remote(fin_send.at[d], fin_recv.at[d], to_other) for d in (RIGHT, LEFT, SELF)]

    def picked(ref, target):
        total = jnp.zeros((BS, BS), F32)
        for slot in range(2):
            weight = (partners[0, slot] == target).astype(F32)
            total = total + ref[slot].astype(F32) * weight
        return total.astype(BF)

    out_row = lax.broadcasted_iota(jnp.int32, (256, 256), 0)
    in_row = lax.broadcasted_iota(jnp.int32, (256, 256), 1)
    perm[...] = (in_row == (out_row & 15) * 16 + (out_row >> 4)).astype(F32).astype(BF)

    n_at = lax.broadcasted_iota(jnp.int32, (half, BS), 0) + core * half
    n_of = lax.broadcasted_iota(jnp.int32, (half, BS), 1)
    choose = (n_at == n_of).astype(F32).astype(BF)
    for copy in loads[2:]:
        copy.wait()
    gsend[pl.ds(0, BS)] = picked(go_ref, left)
    gsend[pl.ds(BS, half)] = nt(choose, picked(gv_ref, left)).astype(BF)
    def turn(n_blocks):
        width = 64 if len(n_blocks) == 1 else 32

        def body(i, carry):
            for n0 in n_blocks:
                for u in range(width // 32):
                    q0 = pl.multiple_of(i * width + u * 32, 32)
                    pair = [
                        traw[core, pl.ds(q0 + 16 * j, 16), pl.ds(n0, 16), :].reshape(256, BS) for j in range(2)
                    ]
                    turned = jnp.dot(
                        perm[...], jnp.concatenate(pair, axis=1), preferred_element_type=F32
                    ).astype(BF)
                    for j in range(2):
                        rows[pl.ds(n0, 16), pl.ds(q0 + 16 * j, 16), :] = (
                            turned[:, j * BS:(j + 1) * BS].reshape(16, 16, BS)
                        )
            return carry

        lax.fori_loop(0, ri // width, body, 0)

    loads[0].wait()
    turn([0])

    pl.semaphore_wait(barrier, 3)
    greens.start()
    siblings[0].start()
    raws[0].start()
    for copy in siblings[1:]:
        copy.start()
    raws[1].start()

    green[pl.ds(0, half)] = nt(choose, picked(go_ref, right)).astype(BF)
    green[pl.ds(2 * half, half)] = nt(choose, picked(go_ref, grid_at)).astype(BF)
    empty = jnp.zeros((BS, BS), BF)

    def doubled(block):
        top = jnp.concatenate([block, empty], axis=1)
        bottom = jnp.concatenate([empty, block], axis=1)
        return jnp.concatenate([top, bottom], axis=0)

    got2[0] = doubled(picked(gv_ref, right))
    got2[2] = doubled(picked(gv_ref, grid_at))
    loads[1].wait()

    def first_product(start, stop, row, many):
        def body(i, carry):
            p0 = pl.multiple_of(i * 8, 8)
            tiles = []
            for j in range(8):
                tiles.append(traw[0, p0 + j])
                tiles.append(traw[1, p0 + j])
            product = nt(green[pl.ds(row, many)], jnp.concatenate(tiles, axis=0)).astype(BF)
            for j in range(8):
                occ[p0 + j, pl.ds(row, many)] = product[:, j * BS:(j + 1) * BS]
            return carry

        lax.fori_loop(start // 8, stop // 8, body, 0)

    def second_product(parts, start, size):
        width = 32 if len(parts) > 1 else min(64, size)

        def body(i, carry):
            for direction, n0 in parts:
                for u in range(width // 16):
                    p0 = pl.multiple_of(i * width + u * 16, 16)
                    pair = [
                        occ[pl.ds(p0, 16), pl.ds(direction * half + n0 + 16 * j, 16), :].reshape(256, BS)
                        for j in range(2)
                    ]
                    turned = jnp.dot(
                        perm[...], jnp.concatenate(pair, axis=1), preferred_element_type=F32
                    ).astype(BF)
                    product = nt(turned, got2[direction]).astype(BF)
                    for j in range(2):
                        trans[direction, pl.ds(n0 + 16 * j, 16), pl.ds(p0, 16), :] = (
                            product[:, j * BS:(j + 1) * BS].reshape(16, 16, BS)
                        )
            return carry

        lax.fori_loop(start // width, (start + size) // width, body, 0)

    for i in range(P_CHUNKS):
        if i == P_CHUNKS - 1:
            turn([16])
            raws[2].start()
        siblings[i].wait_recv()
        a, b = P_BOUNDS[i], P_BOUNDS[i + 1]
        if i == EARLY_CHUNKS:
            greens.wait_recv()
            green[pl.ds(half, half)] = gfar[pl.ds(BS, half)]
            got2[1] = doubled(gfar[pl.ds(0, BS)])
            first_product(0, a, half, 2 * half)
        if i < EARLY_CHUNKS:
            first_product(a, b, 0, half)
        else:
            first_product(a, b, 0, 3 * half)
        second_product([(0, 32)], a, b - a)
        firsts[i].start()
    second_product([(1, 32)], 0, ri)
    seconds[0].start()
    turn([32, 48])
    raws[3].start()
    raws[4].start()

    def wide(ref, at, many):
        return jnp.concatenate([ref[at + j] for j in range(many)], axis=1)

    def contract(jobs, size, clear=False):
        if clear:
            for acc, *_ in jobs:
                acc[...] = jnp.zeros_like(acc)
        groups, rest = divmod(size, 8)

        def add(at, many):
            for acc, x, x0, y, y0 in jobs:
                acc[...] += nt(wide(x, x0 + at, many), wide(y, y0 + at, many))

        def body(i, carry):
            add(8 * i, 8)
            return carry

        if groups > 1:
            lax.fori_loop(0, groups, body, 0)
        elif groups:
            add(0, 8)
        if rest:
            add(8 * groups, rest)

    second_product([(0, 0), (1, 0)], 0, ri)

    def swap_halves(direction, part):
        half_send[direction] = part[theirs, :]
        halves[direction].start()

    def send_back(direction, part, narrow, copy):
        halves[direction].wait_recv()
        narrow[...] = (part[mine, :] + half_recv[direction]).astype(BF)
        copy.start()

    def put(target, total, clear=False):
        for slot in range(2):
            term = total * (partners[0, slot] == target).astype(F32)
            out[slot] = term if clear else out[slot] + term

    def raw_chunk(i):
        a, b = RAW_BOUNDS[i], RAW_BOUNDS[i + 1]
        raws[i].wait_recv()
        jobs = [(acc_right, trans.at[0], a, far, a)]
        if b <= SECOND_BOUNDS[0]:
            jobs.append((part_left, far, a, trans.at[1], a))
        contract(jobs, b - a, clear=i == 0)

    def second_chunk(i):
        a, b = SECOND_BOUNDS[i], SECOND_BOUNDS[i + 1]
        seconds[i].wait_recv()
        contract([(acc_left, rows, a, second, a - SECOND_BOUNDS[0])], b - a, clear=i == 0)

    raw_chunk(0)
    raws[5].start()
    seconds[1].start()
    second_product([(2, 32), (2, 0)], 0, ri)
    raw_chunk(1)
    raws[6].start()
    seconds[2].start()
    contract([(acc_self, trans.at[2], 0, rows, 0)], half, clear=True)
    fin_send[SELF] = acc_self[theirs, :]
    finals[SELF].start()

    raw_chunk(2)
    for copy in firsts:
        copy.wait_recv()
    contract([(part_right, first, 0, rows, FIRST_FROM)], KEEP1, clear=True)
    swap_halves(RIGHT, part_right)
    finals[SELF].wait_recv()
    put(grid_at, acc_self[mine, :] + fin_recv[SELF], clear=True)
    send_back(RIGHT, part_right, back_right_send, back_right)
    raw_chunk(3)
    raw_chunk(4)
    second_chunk(0)
    raw_chunk(5)
    swap_halves(LEFT, part_left)
    second_chunk(1)
    send_back(LEFT, part_left, back_left_send, back_left)
    def last(x, x0, y, y0, many, span):
        left_side = jnp.concatenate([x[x0 + j, span, :] for j in range(many)], axis=1)
        return nt(left_side, wide(y, y0, many))

    a, b = RAW_BOUNDS[-2], RAW_BOUNDS[-1]
    right_end = (trans.at[0], a, far, a, b - a)
    raws[-1].wait_recv()
    fin_send[RIGHT] = acc_right[theirs, :] + last(*right_end, theirs)
    finals[RIGHT].start()
    a, b = SECOND_BOUNDS[-2], SECOND_BOUNDS[-1]
    left_end = (rows, a, second, a - SECOND_BOUNDS[0], b - a)
    seconds[-1].wait_recv()
    fin_send[LEFT] = acc_left[theirs, :] + last(*left_end, theirs)
    finals[LEFT].start()
    acc_right[mine, :] += last(*right_end, mine)
    acc_left[mine, :] += last(*left_end, mine)
    back_right.wait_recv()
    finals[RIGHT].wait_recv()
    put(right, acc_right[mine, :] + ret_right[...].astype(F32) + fin_recv[RIGHT])
    back_left.wait_recv()
    finals[LEFT].wait_recv()
    put(left, acc_left[mine, :] + ret_left[...].astype(F32) + fin_recv[LEFT])

    for copy in [greens, *siblings, *raws, *firsts, *seconds, *halves, back_right, back_left, *finals]:
        copy.wait_send()


COPIES = 1 + 2 * P_CHUNKS + len(RAW_BOUNDS) + len(SECOND_BOUNDS) - 2 + 4 + 3


def on_device(tensor, go_blocks, gv_blocks, partners):
    _, ri, half, _ = tensor.shape
    share = ri // 2
    square = pltpu.VMEM((ri, ri), F32)
    operands = (tensor, go_blocks, gv_blocks, partners)
    placed = [pltpu.with_memory_space_constraint(x, pltpu.HBM) for x in operands]
    narrow = pltpu.VMEM((share, ri), BF)
    blocks = pltpu.VMEM((2, BS, BS), BF)
    green_rows = pltpu.VMEM((BS + half, BS), BF)
    result = pl.pallas_call(
        kernel,
        out_shape=jax.ShapeDtypeStruct((2, share, ri), F32),
        in_specs=[pl.BlockSpec(memory_space=pl.ANY)] * 4,
        out_specs=pl.BlockSpec(memory_space=pltpu.VMEM),
        scratch_shapes=[
            pltpu.VMEM((2, ri, half, BS), BF),
            pltpu.VMEM((half, ri, BS), BF),
            pltpu.VMEM((half - KEEP1, ri, BS), BF),
            pltpu.VMEM((ri, 3 * half, BS), BF),
            pltpu.VMEM((3, half, ri, BS), BF),
            pltpu.VMEM((3, 2 * BS, 2 * BS), BF),
            pltpu.VMEM((256, 256), BF),
            pltpu.VMEM((3 * half, BS), BF),
            pltpu.SMEM((1, 2), jnp.int32),
            blocks, blocks, green_rows, green_rows,
            pltpu.VMEM((KEEP1, ri, BS), BF),
            pltpu.VMEM((KEEP2, ri, BS), BF),
            square, square, square, square, square,
            pltpu.VMEM((2, share, ri), F32),
            pltpu.VMEM((2, share, ri), F32),
            narrow, narrow, narrow, narrow,
            pltpu.VMEM((3, share, ri), F32),
            pltpu.VMEM((3, share, ri), F32),
            pltpu.SemaphoreType.DMA((5,)),
            pltpu.SemaphoreType.DMA((COPIES,)),
            pltpu.SemaphoreType.DMA((COPIES,)),
        ],
        compiler_params=pltpu.CompilerParams(
            collective_id=0, has_side_effects=True, vmem_limit_bytes=52 * 1024 * 1024
        ),
    )(*placed)
    return result[None]


def solution(mesh):
    placed = (
        P("grid", None, "remap", None),
        P("grid", None, None, None),
        P("grid", None, None, None),
        P("grid", None),
    )
    return jax.shard_map(
        on_device,
        mesh=mesh,
        in_specs=placed,
        out_specs=P("grid", None, "remap", None),
        check_vma=False,
    )
```

```python
import jax
import jax.numpy as jnp
from jax import lax
from jax.experimental import pallas as pl
from jax.experimental.pallas import tpu as pltpu
from jax.sharding import PartitionSpec as P

MESH = pl.DeviceIdType.MESH
BF = jnp.bfloat16
F32 = jnp.float32
BS = 128

KEEP1 = 21
KEEP2 = 22
RAW_BOUNDS = (0, 8, 16, 24, 32, 38, 42, 43)
FIRST_FROM = 64 - KEEP1
SECOND_BOUNDS = (42, 52, 60, 64)
P_BOUNDS = (0, 16, 32, 64, 128, 256)
P_CHUNKS = len(P_BOUNDS) - 1
EARLY_CHUNKS = 2

RIGHT, LEFT, SELF = 0, 1, 2


def nt(a, b):
    return lax.dot_general(a, b, (((1,), (1,)), ((), ())), preferred_element_type=F32)


def kernel(
    tensor, go_hbm, gv_hbm, partners_hbm, out,
    traw, rows, far, occ, trans, got2, perm, green, partners, go_ref, gv_ref, gsend, gfar, first, second,
    acc_right, acc_left, acc_self, part_right, part_left,
    half_send, half_recv, back_right_send, back_left_send, ret_right, ret_left,
    fin_send, fin_recv, load_sem, send_sem, recv_sem,
):
    half = rows.shape[0]
    ri = rows.shape[1]
    share = ri // 2
    count = lax.axis_size("grid")
    grid_at = lax.axis_index("grid")
    core = lax.axis_index("remap")
    right = lax.rem(grid_at + 1, count)
    left = lax.rem(grid_at + count - 1, count)
    other = 1 - core

    barrier = pltpu.get_barrier_semaphore()
    for target in ({"grid": left}, {"grid": right}, {"remap": other}):
        pl.semaphore_signal(barrier, inc=1, device_id=target, device_id_type=MESH)

    def loaded(at, n0, size):
        span = pl.ds(n0, size)
        return pltpu.make_async_copy(tensor.at[0, :, span], traw.at[core, :, span], load_sem.at[at])

    loads = [loaded(0, 0, 16), loaded(1, 16, half - 16)]
    loads += [
        pltpu.make_async_copy(partners_hbm, partners, load_sem.at[2]),
        pltpu.make_async_copy(go_hbm.at[0], go_ref, load_sem.at[3]),
        pltpu.make_async_copy(gv_hbm.at[0], gv_ref, load_sem.at[4]),
    ]
    for copy in loads[2:] + loads[:2]:
        copy.start()

    used = [0]

    def remote(source, target, device):
        at = used[0]
        used[0] += 1
        return pltpu.make_async_remote_copy(
            src_ref=source, dst_ref=target, send_sem=send_sem.at[at], recv_sem=recv_sem.at[at],
            device_id=device, device_id_type=MESH,
        )

    to_left, to_right, to_other = {"grid": left}, {"grid": right}, {"remap": other}
    greens = remote(gsend, gfar, to_left)
    theirs = pl.ds(pl.multiple_of(other * share, share), share)
    mine = pl.ds(pl.multiple_of(core * share, share), share)
    p_spans = [pl.ds(a, b - a) for a, b in zip(P_BOUNDS[:-1], P_BOUNDS[1:])]
    siblings = [
        remote(tensor.at[0, span], traw.at[core, span], to_other)
        for span in p_spans
    ]
    raws = [
        remote(rows.at[pl.ds(a, b - a)], far.at[pl.ds(a, b - a)], to_left)
        for a, b in zip(RAW_BOUNDS[:-1], RAW_BOUNDS[1:])
    ]
    firsts = [
        remote(trans.at[0, pl.ds(FIRST_FROM, KEEP1), span], first.at[:, span], to_right)
        for span in p_spans
    ]
    seconds = [
        remote(trans.at[1, pl.ds(a, b - a)], second.at[pl.ds(a - SECOND_BOUNDS[0], b - a)], to_right)
        for a, b in zip(SECOND_BOUNDS[:-1], SECOND_BOUNDS[1:])
    ]
    back_right = remote(back_right_send, ret_right, to_left)
    back_left = remote(back_left_send, ret_left, to_right)
    halves = [remote(half_send.at[d], half_recv.at[d], to_other) for d in (RIGHT, LEFT)]
    finals = [remote(fin_send.at[d], fin_recv.at[d], to_other) for d in (RIGHT, LEFT, SELF)]

    def picked(ref, target):
        total = jnp.zeros((BS, BS), F32)
        for slot in range(2):
            weight = (partners[0, slot] == target).astype(F32)
            total = total + ref[slot].astype(F32) * weight
        return total.astype(BF)

    out_row = lax.broadcasted_iota(jnp.int32, (256, 256), 0)
    in_row = lax.broadcasted_iota(jnp.int32, (256, 256), 1)
    perm[...] = (in_row == (out_row & 15) * 16 + (out_row >> 4)).astype(F32).astype(BF)

    n_at = lax.broadcasted_iota(jnp.int32, (half, BS), 0) + core * half
    n_of = lax.broadcasted_iota(jnp.int32, (half, BS), 1)
    choose = (n_at == n_of).astype(F32).astype(BF)
    for copy in loads[2:]:
        copy.wait()
    gsend[pl.ds(0, BS)] = picked(go_ref, left)
    gsend[pl.ds(BS, half)] = nt(choose, picked(gv_ref, left)).astype(BF)
    def turn(n_blocks):
        width = 128 if len(n_blocks) == 1 else 64

        def body(i, carry):
            for n0 in n_blocks:
                for u in range(width // 32):
                    q0 = pl.multiple_of(i * width + u * 32, 32)
                    pair = [
                        traw[core, pl.ds(q0 + 16 * j, 16), pl.ds(n0, 16), :].reshape(256, BS) for j in range(2)
                    ]
                    turned = jnp.dot(
                        perm[...], jnp.concatenate(pair, axis=1), preferred_element_type=F32
                    ).astype(BF)
                    for j in range(2):
                        rows[pl.ds(n0, 16), pl.ds(q0 + 16 * j, 16), :] = (
                            turned[:, j * BS:(j + 1) * BS].reshape(16, 16, BS)
                        )
            return carry

        lax.fori_loop(0, ri // width, body, 0)

    loads[0].wait()
    turn([0])

    pl.semaphore_wait(barrier, 3)
    greens.start()
    siblings[0].start()
    raws[0].start()
    for copy in siblings[1:]:
        copy.start()
    raws[1].start()

    green[pl.ds(0, half)] = nt(choose, picked(go_ref, right)).astype(BF)
    green[pl.ds(2 * half, half)] = nt(choose, picked(go_ref, grid_at)).astype(BF)
    empty = jnp.zeros((BS, BS), BF)

    def doubled(block):
        top = jnp.concatenate([block, empty], axis=1)
        bottom = jnp.concatenate([empty, block], axis=1)
        return jnp.concatenate([top, bottom], axis=0)

    got2[0] = doubled(picked(gv_ref, right))
    got2[2] = doubled(picked(gv_ref, grid_at))
    loads[1].wait()

    def first_product(start, stop, row, many):
        def body(i, carry):
            p0 = pl.multiple_of(i * 16, 16)
            tiles = []
            for j in range(16):
                tiles.append(traw[0, p0 + j])
                tiles.append(traw[1, p0 + j])
            product = nt(green[pl.ds(row, many)], jnp.concatenate(tiles, axis=0)).astype(BF)
            for j in range(16):
                occ[p0 + j, pl.ds(row, many)] = product[:, j * BS:(j + 1) * BS]
            return carry

        lax.fori_loop(start // 16, stop // 16, body, 0)

    def second_product(parts, start, size):
        width = 64 if len(parts) > 1 else min(128, size)

        def body(i, carry):
            for direction, n0 in parts:
                for u in range(width // 16):
                    p0 = pl.multiple_of(i * width + u * 16, 16)
                    pair = [
                        occ[pl.ds(p0, 16), pl.ds(direction * half + n0 + 16 * j, 16), :].reshape(256, BS)
                        for j in range(2)
                    ]
                    turned = jnp.dot(
                        perm[...], jnp.concatenate(pair, axis=1), preferred_element_type=F32
                    ).astype(BF)
                    product = nt(turned, got2[direction]).astype(BF)
                    for j in range(2):
                        trans[direction, pl.ds(n0 + 16 * j, 16), pl.ds(p0, 16), :] = (
                            product[:, j * BS:(j + 1) * BS].reshape(16, 16, BS)
                        )
            return carry

        lax.fori_loop(start // width, (start + size) // width, body, 0)

    for i in range(P_CHUNKS):
        if i == P_CHUNKS - 1:
            turn([16])
            raws[2].start()
        siblings[i].wait_recv()
        a, b = P_BOUNDS[i], P_BOUNDS[i + 1]
        if i == EARLY_CHUNKS:
            greens.wait_recv()
            green[pl.ds(half, half)] = gfar[pl.ds(BS, half)]
            got2[1] = doubled(gfar[pl.ds(0, BS)])
            first_product(0, a, half, 2 * half)
        if i < EARLY_CHUNKS:
            first_product(a, b, 0, half)
        else:
            first_product(a, b, 0, 3 * half)
        second_product([(0, 32)], a, b - a)
        firsts[i].start()
    second_product([(1, 32)], 0, ri)
    seconds[0].start()
    turn([32, 48])
    raws[3].start()
    raws[4].start()

    def wide(ref, at, many):
        return jnp.concatenate([ref[at + j] for j in range(many)], axis=1)

    def contract(jobs, size, clear=False):
        if clear:
            for acc, *_ in jobs:
                acc[...] = jnp.zeros_like(acc)
        groups, rest = divmod(size, 8)

        def add(at, many):
            for acc, x, x0, y, y0 in jobs:
                acc[...] += nt(wide(x, x0 + at, many), wide(y, y0 + at, many))

        def body(i, carry):
            add(8 * i, 8)
            return carry

        if groups > 1:
            lax.fori_loop(0, groups, body, 0)
        elif groups:
            add(0, 8)
        if rest:
            add(8 * groups, rest)

    second_product([(0, 0), (1, 0)], 0, ri)

    def swap_halves(direction, part):
        half_send[direction] = part[theirs, :]
        halves[direction].start()

    def send_back(direction, part, narrow, copy):
        halves[direction].wait_recv()
        narrow[...] = (part[mine, :] + half_recv[direction]).astype(BF)
        copy.start()

    def put(target, total, clear=False):
        for slot in range(2):
            term = total * (partners[0, slot] == target).astype(F32)
            out[slot] = term if clear else out[slot] + term

    def raw_chunk(i):
        a, b = RAW_BOUNDS[i], RAW_BOUNDS[i + 1]
        raws[i].wait_recv()
        jobs = [(acc_right, trans.at[0], a, far, a)]
        if b <= SECOND_BOUNDS[0]:
            jobs.append((part_left, far, a, trans.at[1], a))
        contract(jobs, b - a, clear=i == 0)

    def second_chunk(i):
        a, b = SECOND_BOUNDS[i], SECOND_BOUNDS[i + 1]
        seconds[i].wait_recv()
        contract([(acc_left, rows, a, second, a - SECOND_BOUNDS[0])], b - a, clear=i == 0)

    raw_chunk(0)
    raws[5].start()
    seconds[1].start()
    second_product([(2, 32), (2, 0)], 0, ri)
    raw_chunk(1)
    raws[6].start()
    seconds[2].start()
    contract([(acc_self, trans.at[2], 0, rows, 0)], half, clear=True)
    fin_send[SELF] = acc_self[theirs, :]
    finals[SELF].start()

    raw_chunk(2)
    for copy in firsts:
        copy.wait_recv()
    contract([(part_right, first, 0, rows, FIRST_FROM)], KEEP1, clear=True)
    swap_halves(RIGHT, part_right)
    finals[SELF].wait_recv()
    put(grid_at, acc_self[mine, :] + fin_recv[SELF], clear=True)
    send_back(RIGHT, part_right, back_right_send, back_right)
    raw_chunk(3)
    raw_chunk(4)
    second_chunk(0)
    raw_chunk(5)
    swap_halves(LEFT, part_left)
    second_chunk(1)
    send_back(LEFT, part_left, back_left_send, back_left)
    def last(x, x0, y, y0, many, span):
        left_side = jnp.concatenate([x[x0 + j, span, :] for j in range(many)], axis=1)
        return nt(left_side, wide(y, y0, many))

    a, b = RAW_BOUNDS[-2], RAW_BOUNDS[-1]
    right_end = (trans.at[0], a, far, a, b - a)
    raws[-1].wait_recv()
    fin_send[RIGHT] = acc_right[theirs, :] + last(*right_end, theirs)
    finals[RIGHT].start()
    a, b = SECOND_BOUNDS[-2], SECOND_BOUNDS[-1]
    left_end = (rows, a, second, a - SECOND_BOUNDS[0], b - a)
    seconds[-1].wait_recv()
    fin_send[LEFT] = acc_left[theirs, :] + last(*left_end, theirs)
    finals[LEFT].start()
    acc_right[mine, :] += last(*right_end, mine)
    acc_left[mine, :] += last(*left_end, mine)
    back_right.wait_recv()
    finals[RIGHT].wait_recv()
    put(right, acc_right[mine, :] + ret_right[...].astype(F32) + fin_recv[RIGHT])
    back_left.wait_recv()
    finals[LEFT].wait_recv()
    put(left, acc_left[mine, :] + ret_left[...].astype(F32) + fin_recv[LEFT])

    for copy in [greens, *siblings, *raws, *firsts, *seconds, *halves, back_right, back_left, *finals]:
        copy.wait_send()


COPIES = 1 + 2 * P_CHUNKS + len(RAW_BOUNDS) + len(SECOND_BOUNDS) - 2 + 4 + 3


def on_device(tensor, go_blocks, gv_blocks, partners):
    _, ri, half, _ = tensor.shape
    share = ri // 2
    square = pltpu.VMEM((ri, ri), F32)
    operands = (tensor, go_blocks, gv_blocks, partners)
    placed = [pltpu.with_memory_space_constraint(x, pltpu.HBM) for x in operands]
    narrow = pltpu.VMEM((share, ri), BF)
    blocks = pltpu.VMEM((2, BS, BS), BF)
    green_rows = pltpu.VMEM((BS + half, BS), BF)
    result = pl.pallas_call(
        kernel,
        out_shape=jax.ShapeDtypeStruct((2, share, ri), F32),
        in_specs=[pl.BlockSpec(memory_space=pl.ANY)] * 4,
        out_specs=pl.BlockSpec(memory_space=pltpu.VMEM),
        scratch_shapes=[
            pltpu.VMEM((2, ri, half, BS), BF),
            pltpu.VMEM((half, ri, BS), BF),
            pltpu.VMEM((half - KEEP1, ri, BS), BF),
            pltpu.VMEM((ri, 3 * half, BS), BF),
            pltpu.VMEM((3, half, ri, BS), BF),
            pltpu.VMEM((3, 2 * BS, 2 * BS), BF),
            pltpu.VMEM((256, 256), BF),
            pltpu.VMEM((3 * half, BS), BF),
            pltpu.SMEM((1, 2), jnp.int32),
            blocks, blocks, green_rows, green_rows,
            pltpu.VMEM((KEEP1, ri, BS), BF),
            pltpu.VMEM((KEEP2, ri, BS), BF),
            square, square, square, square, square,
            pltpu.VMEM((2, share, ri), F32),
            pltpu.VMEM((2, share, ri), F32),
            narrow, narrow, narrow, narrow,
            pltpu.VMEM((3, share, ri), F32),
            pltpu.VMEM((3, share, ri), F32),
            pltpu.SemaphoreType.DMA((5,)),
            pltpu.SemaphoreType.DMA((COPIES,)),
            pltpu.SemaphoreType.DMA((COPIES,)),
        ],
        compiler_params=pltpu.CompilerParams(
            collective_id=0, has_side_effects=True, vmem_limit_bytes=52 * 1024 * 1024
        ),
    )(*placed)
    return result[None]


def solution(mesh):
    placed = (
        P("grid", None, "remap", None),
        P("grid", None, None, None),
        P("grid", None, None, None),
        P("grid", None),
    )
    return jax.shard_map(
        on_device,
        mesh=mesh,
        in_specs=placed,
        out_specs=P("grid", None, "remap", None),
        check_vma=False,
    )
```

```python
import jax
import jax.numpy as jnp
from jax import lax
from jax.experimental import pallas as pl
from jax.experimental.pallas import tpu as pltpu
from jax.sharding import PartitionSpec as P

MESH = pl.DeviceIdType.MESH
BF = jnp.bfloat16
F32 = jnp.float32
BS = 128

KEEP1 = 21
KEEP2 = 22
RAW_BOUNDS = (0, 8, 16, 24, 32, 40, 42, 43)
FIRST_FROM = 64 - KEEP1
SECOND_BOUNDS = (42, 54, 62, 64)
P_BOUNDS = (0, 16, 32, 64, 128, 256)
P_CHUNKS = len(P_BOUNDS) - 1
EARLY_CHUNKS = 2

RIGHT, LEFT, SELF = 0, 1, 2


def nt(a, b):
    return lax.dot_general(a, b, (((1,), (1,)), ((), ())), preferred_element_type=F32)


def kernel(
    tensor, go_hbm, gv_hbm, partners_hbm, out,
    traw, rows, far, occ, trans, got2, perm, green, partners, go_ref, gv_ref, gsend, gfar, first, second,
    acc_right, acc_left, acc_self, part_right, part_left,
    half_send, half_recv, back_right_send, back_left_send, ret_right, ret_left,
    fin_send, fin_recv, load_sem, send_sem, recv_sem,
):
    half = rows.shape[0]
    ri = rows.shape[1]
    share = ri // 2
    count = lax.axis_size("grid")
    grid_at = lax.axis_index("grid")
    core = lax.axis_index("remap")
    right = lax.rem(grid_at + 1, count)
    left = lax.rem(grid_at + count - 1, count)
    other = 1 - core

    barrier = pltpu.get_barrier_semaphore()
    for target in ({"grid": left}, {"grid": right}, {"remap": other}):
        pl.semaphore_signal(barrier, inc=1, device_id=target, device_id_type=MESH)

    def loaded(at, n0, size):
        span = pl.ds(n0, size)
        return pltpu.make_async_copy(tensor.at[0, :, span], traw.at[core, :, span], load_sem.at[at])

    loads = [loaded(0, 0, 16), loaded(1, 16, half - 16)]
    loads += [
        pltpu.make_async_copy(partners_hbm, partners, load_sem.at[2]),
        pltpu.make_async_copy(go_hbm.at[0], go_ref, load_sem.at[3]),
        pltpu.make_async_copy(gv_hbm.at[0], gv_ref, load_sem.at[4]),
    ]
    for copy in loads[2:] + loads[:2]:
        copy.start()

    used = [0]

    def remote(source, target, device):
        at = used[0]
        used[0] += 1
        return pltpu.make_async_remote_copy(
            src_ref=source, dst_ref=target, send_sem=send_sem.at[at], recv_sem=recv_sem.at[at],
            device_id=device, device_id_type=MESH,
        )

    to_left, to_right, to_other = {"grid": left}, {"grid": right}, {"remap": other}
    greens = remote(gsend, gfar, to_left)
    theirs = pl.ds(pl.multiple_of(other * share, share), share)
    mine = pl.ds(pl.multiple_of(core * share, share), share)
    p_spans = [pl.ds(a, b - a) for a, b in zip(P_BOUNDS[:-1], P_BOUNDS[1:])]
    siblings = [
        remote(tensor.at[0, span], traw.at[core, span], to_other)
        for span in p_spans
    ]
    raws = [
        remote(rows.at[pl.ds(a, b - a)], far.at[pl.ds(a, b - a)], to_left)
        for a, b in zip(RAW_BOUNDS[:-1], RAW_BOUNDS[1:])
    ]
    firsts = [
        remote(trans.at[0, pl.ds(FIRST_FROM, KEEP1), span], first.at[:, span], to_right)
        for span in p_spans
    ]
    seconds = [
        remote(trans.at[1, pl.ds(a, b - a)], second.at[pl.ds(a - SECOND_BOUNDS[0], b - a)], to_right)
        for a, b in zip(SECOND_BOUNDS[:-1], SECOND_BOUNDS[1:])
    ]
    back_right = remote(back_right_send, ret_right, to_left)
    back_left = remote(back_left_send, ret_left, to_right)
    halves = [remote(half_send.at[d], half_recv.at[d], to_other) for d in (RIGHT, LEFT)]
    finals = [remote(fin_send.at[d], fin_recv.at[d], to_other) for d in (RIGHT, LEFT, SELF)]

    def picked(ref, target):
        total = jnp.zeros((BS, BS), F32)
        for slot in range(2):
            weight = (partners[0, slot] == target).astype(F32)
            total = total + ref[slot].astype(F32) * weight
        return total.astype(BF)

    out_row = lax.broadcasted_iota(jnp.int32, (256, 256), 0)
    in_row = lax.broadcasted_iota(jnp.int32, (256, 256), 1)
    perm[...] = (in_row == (out_row & 15) * 16 + (out_row >> 4)).astype(F32).astype(BF)

    n_at = lax.broadcasted_iota(jnp.int32, (half, BS), 0) + core * half
    n_of = lax.broadcasted_iota(jnp.int32, (half, BS), 1)
    choose = (n_at == n_of).astype(F32).astype(BF)
    for copy in loads[2:]:
        copy.wait()
    gsend[pl.ds(0, BS)] = picked(go_ref, left)
    gsend[pl.ds(BS, half)] = nt(choose, picked(gv_ref, left)).astype(BF)
    def turn(n_blocks):
        width = 128 if len(n_blocks) == 1 else 64

        def body(i, carry):
            for n0 in n_blocks:
                for u in range(width // 32):
                    q0 = pl.multiple_of(i * width + u * 32, 32)
                    pair = [
                        traw[core, pl.ds(q0 + 16 * j, 16), pl.ds(n0, 16), :].reshape(256, BS) for j in range(2)
                    ]
                    turned = jnp.dot(
                        perm[...], jnp.concatenate(pair, axis=1), preferred_element_type=F32
                    ).astype(BF)
                    for j in range(2):
                        rows[pl.ds(n0, 16), pl.ds(q0 + 16 * j, 16), :] = (
                            turned[:, j * BS:(j + 1) * BS].reshape(16, 16, BS)
                        )
            return carry

        lax.fori_loop(0, ri // width, body, 0)

    loads[0].wait()
    turn([0])

    pl.semaphore_wait(barrier, 3)
    greens.start()
    siblings[0].start()
    raws[0].start()
    for copy in siblings[1:]:
        copy.start()
    raws[1].start()

    green[pl.ds(0, half)] = nt(choose, picked(go_ref, right)).astype(BF)
    green[pl.ds(2 * half, half)] = nt(choose, picked(go_ref, grid_at)).astype(BF)
    empty = jnp.zeros((BS, BS), BF)

    def doubled(block):
        top = jnp.concatenate([block, empty], axis=1)
        bottom = jnp.concatenate([empty, block], axis=1)
        return jnp.concatenate([top, bottom], axis=0)

    got2[0] = doubled(picked(gv_ref, right))
    got2[2] = doubled(picked(gv_ref, grid_at))
    loads[1].wait()

    def first_product(start, stop, row, many):
        def body(i, carry):
            p0 = pl.multiple_of(i * 16, 16)
            tiles = []
            for j in range(16):
                tiles.append(traw[0, p0 + j])
                tiles.append(traw[1, p0 + j])
            product = nt(green[pl.ds(row, many)], jnp.concatenate(tiles, axis=0)).astype(BF)
            for j in range(16):
                occ[p0 + j, pl.ds(row, many)] = product[:, j * BS:(j + 1) * BS]
            return carry

        lax.fori_loop(start // 16, stop // 16, body, 0)

    def second_product(parts, start, size):
        width = 64 if len(parts) > 1 else min(128, size)

        def body(i, carry):
            for direction, n0 in parts:
                for u in range(width // 16):
                    p0 = pl.multiple_of(i * width + u * 16, 16)
                    pair = [
                        occ[pl.ds(p0, 16), pl.ds(direction * half + n0 + 16 * j, 16), :].reshape(256, BS)
                        for j in range(2)
                    ]
                    turned = jnp.dot(
                        perm[...], jnp.concatenate(pair, axis=1), preferred_element_type=F32
                    ).astype(BF)
                    product = nt(turned, got2[direction]).astype(BF)
                    for j in range(2):
                        trans[direction, pl.ds(n0 + 16 * j, 16), pl.ds(p0, 16), :] = (
                            product[:, j * BS:(j + 1) * BS].reshape(16, 16, BS)
                        )
            return carry

        lax.fori_loop(start // width, (start + size) // width, body, 0)

    for i in range(P_CHUNKS):
        if i == P_CHUNKS - 1:
            turn([16])
            raws[2].start()
        siblings[i].wait_recv()
        a, b = P_BOUNDS[i], P_BOUNDS[i + 1]
        if i == EARLY_CHUNKS:
            greens.wait_recv()
            green[pl.ds(half, half)] = gfar[pl.ds(BS, half)]
            got2[1] = doubled(gfar[pl.ds(0, BS)])
            first_product(0, a, half, 2 * half)
        if i < EARLY_CHUNKS:
            first_product(a, b, 0, half)
        else:
            first_product(a, b, 0, 3 * half)
        second_product([(0, 32)], a, b - a)
        firsts[i].start()
    second_product([(1, 32)], 0, ri)
    seconds[0].start()
    turn([32, 48])
    raws[3].start()
    raws[4].start()

    def wide(ref, at, many):
        return jnp.concatenate([ref[at + j] for j in range(many)], axis=1)

    def contract(jobs, size, clear=False):
        if clear:
            for acc, *_ in jobs:
                acc[...] = jnp.zeros_like(acc)
        groups, rest = divmod(size, 8)

        def add(at, many):
            for acc, x, x0, y, y0 in jobs:
                acc[...] += nt(wide(x, x0 + at, many), wide(y, y0 + at, many))

        def body(i, carry):
            add(8 * i, 8)
            return carry

        if groups > 1:
            lax.fori_loop(0, groups, body, 0)
        elif groups:
            add(0, 8)
        if rest:
            add(8 * groups, rest)

    second_product([(0, 0), (1, 0)], 0, ri)

    def swap_halves(direction, part):
        half_send[direction] = part[theirs, :]
        halves[direction].start()

    def send_back(direction, part, narrow, copy):
        halves[direction].wait_recv()
        narrow[...] = (part[mine, :] + half_recv[direction]).astype(BF)
        copy.start()

    def put(target, total, clear=False):
        for slot in range(2):
            term = total * (partners[0, slot] == target).astype(F32)
            out[slot] = term if clear else out[slot] + term

    def raw_chunk(i):
        a, b = RAW_BOUNDS[i], RAW_BOUNDS[i + 1]
        raws[i].wait_recv()
        jobs = [(acc_right, trans.at[0], a, far, a)]
        if b <= SECOND_BOUNDS[0]:
            jobs.append((part_left, far, a, trans.at[1], a))
        contract(jobs, b - a, clear=i == 0)

    def second_chunk(i):
        a, b = SECOND_BOUNDS[i], SECOND_BOUNDS[i + 1]
        seconds[i].wait_recv()
        contract([(acc_left, rows, a, second, a - SECOND_BOUNDS[0])], b - a, clear=i == 0)

    raw_chunk(0)
    raws[5].start()
    seconds[1].start()
    second_product([(2, 32), (2, 0)], 0, ri)
    raw_chunk(1)
    raws[6].start()
    seconds[2].start()
    contract([(acc_self, trans.at[2], 0, rows, 0)], half, clear=True)
    fin_send[SELF] = acc_self[theirs, :]
    finals[SELF].start()

    raw_chunk(2)
    for copy in firsts:
        copy.wait_recv()
    contract([(part_right, first, 0, rows, FIRST_FROM)], KEEP1, clear=True)
    swap_halves(RIGHT, part_right)
    finals[SELF].wait_recv()
    put(grid_at, acc_self[mine, :] + fin_recv[SELF], clear=True)
    send_back(RIGHT, part_right, back_right_send, back_right)
    raw_chunk(3)
    raw_chunk(4)
    second_chunk(0)
    raw_chunk(5)
    swap_halves(LEFT, part_left)
    second_chunk(1)
    send_back(LEFT, part_left, back_left_send, back_left)
    def last(x, x0, y, y0, many, span):
        left_side = jnp.concatenate([x[x0 + j, span, :] for j in range(many)], axis=1)
        return nt(left_side, wide(y, y0, many))

    a, b = RAW_BOUNDS[-2], RAW_BOUNDS[-1]
    right_end = (trans.at[0], a, far, a, b - a)
    raws[-1].wait_recv()
    fin_send[RIGHT] = acc_right[theirs, :] + last(*right_end, theirs)
    finals[RIGHT].start()
    a, b = SECOND_BOUNDS[-2], SECOND_BOUNDS[-1]
    left_end = (rows, a, second, a - SECOND_BOUNDS[0], b - a)
    seconds[-1].wait_recv()
    fin_send[LEFT] = acc_left[theirs, :] + last(*left_end, theirs)
    finals[LEFT].start()
    acc_right[mine, :] += last(*right_end, mine)
    acc_left[mine, :] += last(*left_end, mine)
    back_right.wait_recv()
    finals[RIGHT].wait_recv()
    put(right, acc_right[mine, :] + ret_right[...].astype(F32) + fin_recv[RIGHT])
    back_left.wait_recv()
    finals[LEFT].wait_recv()
    put(left, acc_left[mine, :] + ret_left[...].astype(F32) + fin_recv[LEFT])

    for copy in [greens, *siblings, *raws, *firsts, *seconds, *halves, back_right, back_left, *finals]:
        copy.wait_send()


COPIES = 1 + 2 * P_CHUNKS + len(RAW_BOUNDS) + len(SECOND_BOUNDS) - 2 + 4 + 3


def on_device(tensor, go_blocks, gv_blocks, partners):
    _, ri, half, _ = tensor.shape
    share = ri // 2
    square = pltpu.VMEM((ri, ri), F32)
    operands = (tensor, go_blocks, gv_blocks, partners)
    placed = [pltpu.with_memory_space_constraint(x, pltpu.HBM) for x in operands]
    narrow = pltpu.VMEM((share, ri), BF)
    blocks = pltpu.VMEM((2, BS, BS), BF)
    green_rows = pltpu.VMEM((BS + half, BS), BF)
    result = pl.pallas_call(
        kernel,
        out_shape=jax.ShapeDtypeStruct((2, share, ri), F32),
        in_specs=[pl.BlockSpec(memory_space=pl.ANY)] * 4,
        out_specs=pl.BlockSpec(memory_space=pltpu.VMEM),
        scratch_shapes=[
            pltpu.VMEM((2, ri, half, BS), BF),
            pltpu.VMEM((half, ri, BS), BF),
            pltpu.VMEM((half - KEEP1, ri, BS), BF),
            pltpu.VMEM((ri, 3 * half, BS), BF),
            pltpu.VMEM((3, half, ri, BS), BF),
            pltpu.VMEM((3, 2 * BS, 2 * BS), BF),
            pltpu.VMEM((256, 256), BF),
            pltpu.VMEM((3 * half, BS), BF),
            pltpu.SMEM((1, 2), jnp.int32),
            blocks, blocks, green_rows, green_rows,
            pltpu.VMEM((KEEP1, ri, BS), BF),
            pltpu.VMEM((KEEP2, ri, BS), BF),
            square, square, square, square, square,
            pltpu.VMEM((2, share, ri), F32),
            pltpu.VMEM((2, share, ri), F32),
            narrow, narrow, narrow, narrow,
            pltpu.VMEM((3, share, ri), F32),
            pltpu.VMEM((3, share, ri), F32),
            pltpu.SemaphoreType.DMA((5,)),
            pltpu.SemaphoreType.DMA((COPIES,)),
            pltpu.SemaphoreType.DMA((COPIES,)),
        ],
        compiler_params=pltpu.CompilerParams(
            collective_id=0, has_side_effects=True, vmem_limit_bytes=52 * 1024 * 1024
        ),
    )(*placed)
    return result[None]


def solution(mesh):
    placed = (
        P("grid", None, "remap", None),
        P("grid", None, None, None),
        P("grid", None, None, None),
        P("grid", None),
    )
    return jax.shard_map(
        on_device,
        mesh=mesh,
        in_specs=placed,
        out_specs=P("grid", None, "remap", None),
        check_vma=False,
    )
```
